256 devices in a mesh: dp: 4 (over x_lo, core), eig: 64 (over z, x_hi, y).
Axes of the slice: x: 4 (x_hi: 2, x_lo: 2; x = x_hi * 2 + x_lo), y: 4, z: 8, core: 2. Of those that a mesh axis runs over, the one named last changes fastest.
Arguments:
- activations: bfloat16 [8192, 5120], P(('dp', 'eig')), may hold values from -6 to 6
- out_grads: bfloat16 [13824, 8192], P('eig', 'dp'), may hold values from -6 to 6
- basis_in: bfloat16 [5120, 5120], P('eig'), may hold values from -0.078125 to 0.078125
- basis_out: bfloat16 [13824, 13824], P('eig'), may hold values from -0.0546875 to 0.0546875
- block_ids: int32 [8], replicated, may hold values from 0 to 107, as said below
- seq_lens: int32 [8], P('dp'), may hold values from 128 to 1024, as said below
- query_grads: bfloat16 [32, 5120, 1024], P('dp', 'eig'), may hold values from -7.6293945e-05 to 7.6293945e-05
Outputs:
- scores: float32 [8, 32], P(None, 'dp')
The draws below stay inside these ranges and needn't reach their ends.
Inputs may be any that keep to these rules, and one draw needn't show every extreme that they name: `block_ids`: distinct block numbers; blocks of 128 columns of basis_out. `seq_lens`: slots of a sequence from its count on are padding.
All inputs are finite; a program needn't handle non-finite values.
Results may differ from the reference program's by a relative error of at most 0.0052.
Values may be sent and summed in bfloat16 or wider, within the bound.
No kernel may reach another device: no remote copies, remote signals or barrier semaphores. Data moves between devices by JAX's collectives and lax.ppermute only.
A program may use at most 128 MiB of HBM per device.

```python
import jax
import jax.numpy as jnp

D = 5120
FF = 13824
BLOCK = 128
NSEL = 8
LEN = 1024
QUERIES = 32
SELW = 1024
SEQS = 8
TOKENS = 8192


def draw_block_ids(key, part):
    first_key, second_key = jax.random.split(key)
    blocks_all = FF // BLOCK
    leading = jax.random.permutation(first_key, blocks_all - 1)[:NSEL - 1].astype(jnp.int32)
    chosen = jnp.concatenate([leading, jnp.array([blocks_all - 1], dtype=jnp.int32)])
    order = jax.random.permutation(second_key, NSEL)
    return chosen[order].astype(jnp.int32)


def draw_seq_lens(key, part):
    first_key, second_key, third_key = jax.random.split(key, 3)
    counts = jax.random.randint(first_key, (SEQS,), LEN // 8, LEN + 1).astype(jnp.int32)
    longest = jax.random.randint(second_key, (), 0, SEQS).astype(jnp.int32)
    offset = jax.random.randint(third_key, (), 1, SEQS).astype(jnp.int32)
    shortest = (longest + offset) % SEQS
    places = jnp.arange(SEQS, dtype=jnp.int32)
    counts = jnp.where(places == longest, LEN, counts)
    counts = jnp.where(places == shortest, LEN // 8, counts)
    return counts.astype(jnp.int32)


def block_levels(rng, shape, pieces, least, top_value):
    factor_of = 1.0
    for dim, parts in pieces:
        steps = jax.random.uniform(jax.random.fold_in(jax.random.fold_in(rng, 6), dim), (parts,), jnp.float32, least / len(pieces), top_value / len(pieces))
        factor_of = factor_of * jnp.repeat(jnp.exp(steps), shape[dim] // parts).reshape((-1,) + (1,) * (len(shape) - 1 - dim))
    return factor_of


def scatter_about(key, shape, width, most, pieces=(), kind=jnp.bfloat16):
    loudness = block_levels(key, shape, pieces, -0.22, 0.18) if pieces else 1.0
    values = jax.random.normal(key, shape, jnp.float32) * width * loudness
    return jnp.minimum(jnp.maximum(values, -most), most).astype(kind)


def setup_inputs(seed: int = 0) -> dict:
    key_of = jax.random.split(jax.random.key(seed), 8)
    return {
        "activations": scatter_about(key_of[0], (TOKENS, D), 1.0, 6.0, ((0, 256),)),
        "out_grads": scatter_about(key_of[1], (FF, TOKENS), 1.0, 6.0, ((0, 64), (1, 4))),
        "basis_in": scatter_about(key_of[2], (D, D), D ** -0.5, 0.078125, ((0, 64),)),
        "basis_out": scatter_about(key_of[3], (FF, FF), FF ** -0.5, 0.0546875, ((0, 64),)),
        "block_ids": draw_block_ids(jax.random.fold_in(key_of[7], 71), 0),
        "seq_lens": draw_seq_lens(jax.random.fold_in(key_of[7], 71), 0),
        "query_grads": scatter_about(key_of[6], (QUERIES, D, SELW), (LEN * SELW * D) ** -0.5, 7.62939453125e-05, ((0, 4), (1, 64))),
    }


def reference(activations, out_grads, basis_in, basis_out, block_ids, seq_lens, query_grads):
    rotated_act = jnp.dot(basis_in, activations.T, preferred_element_type=jnp.float32).astype(jnp.bfloat16)
    columns = (block_ids[:, None] * BLOCK + jnp.arange(BLOCK, dtype=jnp.int32)[None, :]).reshape(-1).astype(jnp.int32)
    chosen_basis = jnp.take(basis_out, columns, axis=1)
    summed_grad = jnp.dot(chosen_basis.T, out_grads, preferred_element_type=jnp.float32).astype(jnp.bfloat16)
    live_slots = jnp.arange(LEN, dtype=jnp.int32)[None, :] < seq_lens[:, None]
    rotated_grad = jnp.where(live_slots.reshape(1, SEQS * LEN), summed_grad, jnp.zeros((), jnp.bfloat16))
    grad_blocks = rotated_grad.reshape(SELW, SEQS, LEN).astype(jnp.float32)
    act_blocks = rotated_act.reshape(D, SEQS, LEN).astype(jnp.float32)
    seq_grads = jnp.einsum("ksl,isl->sik", grad_blocks, act_blocks).astype(jnp.bfloat16)
    scores = jnp.einsum("sik,qik->sq", seq_grads.astype(jnp.float32), query_grads.astype(jnp.float32))
    return scores
```

```python
import jax
import jax.numpy as jnp
import numpy as np
from jax import lax
from jax.sharding import Mesh, PartitionSpec as P

BLOCK = 128
NSEL = 8
LEN = 1024
BF = jnp.bfloat16
F32 = jnp.float32


def spread(x, axes, count):
    return lax.all_to_all(
        jnp.broadcast_to(x[None], (count,) + x.shape), axes, split_axis=0, concat_axis=0, tiled=True
    )


def dot(a, b, ca, cb):
    return lax.dot_general(a, b, (((ca,), (cb,)), ((), ())), preferred_element_type=F32)


def per_device(activations, out_grads, basis_in, basis_out, block_ids, seq_lens, query_grads):
    chosen = jnp.concatenate(
        [
            lax.dynamic_slice_in_dim(basis_out, block_ids[number] * BLOCK, BLOCK, 1)
            for number in range(NSEL)
        ],
        axis=1,
    )
    y = lax.axis_index("y")
    rows = out_grads.shape[0]
    grads_out = out_grads.reshape(rows, 16, 4, 32).transpose(2, 0, 1, 3).reshape(4, rows, 512)
    grads = lax.all_to_all(grads_out, "y", split_axis=0, concat_axis=0, tiled=True)
    chosen_all = spread(chosen, "y", 4)
    partial = dot(chosen_all.reshape(4 * rows, 1024), grads.reshape(4 * rows, 512), 0, 0).astype(BF)
    parts = lax.all_to_all(partial.reshape(16, 64, 512), ("xh", "z"), split_axis=0, concat_axis=0, tiled=True)
    summed = jnp.sum(parts.astype(F32), axis=0).astype(BF)
    col = lax.broadcasted_iota(jnp.int32, (1, 512), 1)
    pos = (col // 32 % 8) * 128 + y * 32 + col % 32
    limit = jnp.where(col < 256, seq_lens[0], seq_lens[1])
    rotated = jnp.where(pos < limit, summed, jnp.zeros((), BF))
    rotated_all = spread(rotated, "z", 8).reshape(512, 512)

    acts = lax.all_gather(activations, "xh", axis=0, tiled=True)
    acts = lax.all_gather(acts, "z", axis=0, tiled=True)
    basis = spread(basis_in, "y", 4).reshape(320, -1)
    rotated_act = dot(basis, acts, 1, 1).astype(BF)
    act_all = lax.all_gather(rotated_act, "xh", axis=0, tiled=True)

    seq_parts = jnp.stack(
        [dot(act_all[:, s * 256 : s * 256 + 256], rotated_all[:, s * 256 : s * 256 + 256], 1, 1) for s in range(2)]
    ).astype(BF)
    sent = seq_parts.reshape(2, 8, 80, 512).transpose(1, 0, 2, 3)
    got = lax.all_to_all(sent, ("xh", "y"), split_axis=0, concat_axis=0, tiled=True)
    seq_grads = jnp.sum(got.reshape(2, 4, 2, 80, 512).astype(F32), axis=1).astype(BF)
    every = lax.all_gather(seq_grads, ("xl", "core"), axis=1, tiled=True)
    queries = query_grads.reshape(8, 80, 2, 512)
    scores = sum(
        jnp.einsum("sik,qik->sq", every[h], queries[:, :, h], preferred_element_type=F32) for h in range(2)
    )
    scores = jnp.sum(spread(scores, ("xh", "y"), 8), axis=0)
    return jnp.sum(spread(scores, "z", 8), axis=0)


def solution(mesh):
    fine = Mesh(mesh.devices.reshape(2, 2, 8, 2, 4), ("xl", "core", "z", "xh", "y"))
    dp, eig = ("xl", "core"), ("z", "xh", "y")
    in_specs = (
        P(dp + eig, None),
        P(eig, dp),
        P(eig, None),
        P(eig, None),
        P(),
        P(dp),
        P(dp, eig, None),
    )
    return jax.shard_map(
        per_device, mesh=fine, in_specs=in_specs, out_specs=P(None, dp), check_vma=False
    )
```

```python
import jax
import jax.numpy as jnp
from jax import lax
from jax.experimental import pallas as pl
from jax.experimental.pallas import tpu as pltpu
from jax.sharding import Mesh, PartitionSpec as P

BLOCK = 128
LEN = 1024
BF = jnp.bfloat16
F32 = jnp.float32
SIZES = {"xl": 2, "core": 2, "z": 8, "xh": 2, "y": 4}
DY = (0, 1, -1, 2)
VMEM = pl.BlockSpec(memory_space=pltpu.VMEM)
SMEM = pl.BlockSpec(memory_space=pltpu.SMEM)
ROOM = pltpu.CompilerParams(vmem_limit_bytes=48 * 1024 * 1024)


def shift(x, **by):
    axes = tuple(by)
    count = 1
    for a in axes:
        count *= SIZES[a]
    pairs = []
    for source in range(count):
        rest, target, scale = source, 0, 1
        for a in reversed(axes):
            target += (rest % SIZES[a] + by[a]) % SIZES[a] * scale
            rest //= SIZES[a]
            scale *= SIZES[a]
        pairs.append((source, target))
    return lax.ppermute(x, axes, pairs)


def spread(x, axes, count):
    return lax.all_to_all(
        jnp.broadcast_to(x[None], (count,) + x.shape), axes, split_axis=0, concat_axis=0, tiled=True
    )


def dot(a, b, ca, cb):
    return lax.dot_general(a, b, (((ca,), (cb,)), ((), ())), preferred_element_type=F32)


def pick_kernel(s_ref, b0, b1, g_ref, c_ref, *o_refs):
    c_ref[:, :128] = b0[...]
    c_ref[:, 128:] = b1[...]
    y = s_ref[8]
    xh = pl.program_id(0) // 2
    lane = lax.broadcasted_iota(jnp.int32, (1, 128), 1) // 32
    cols = [g_ref[:, pl.ds(pl.multiple_of((2 * j + xh) * 128, 128), 128)].astype(F32) for j in range(4)]
    for n, dy in enumerate(DY):
        total = None
        for j in range(4):
            moved = pltpu.roll(cols[j], ((j - dy - y + 8) % 4) * 32, 1)
            total = moved if total is None else jnp.where(lane == j, moved, total)
        o_refs[n][...] = total.astype(BF)


def pick(block_ids, y, basis_out, out_grads):
    rows, tokens = out_grads.shape
    scalars = jnp.concatenate([block_ids, y[None].astype(jnp.int32)])
    spec = pltpu.PrefetchScalarGridSpec(
        num_scalar_prefetch=1,
        grid=(4,),
        in_specs=[
            pl.BlockSpec((rows, BLOCK), lambda g, s: (0, s[2 * g])),
            pl.BlockSpec((rows, BLOCK), lambda g, s: (0, s[2 * g + 1])),
            pl.BlockSpec((rows, 1024), lambda g, s: (0, g % 2)),
        ],
        out_specs=[pl.BlockSpec((rows, 256), lambda g, s: (0, g))]
        + [pl.BlockSpec((rows, 128), lambda g, s: (0, g))] * 4,
    )
    return pl.pallas_call(
        pick_kernel,
        grid_spec=spec,
        out_shape=[jax.ShapeDtypeStruct((rows, 1024), BF)] + [jax.ShapeDtypeStruct((rows, 512), BF)] * 4,
        compiler_params=ROOM,
        name="pick",
    )(scalars, basis_out, basis_out, out_grads)


def grads_kernel(c0, c1, c2, c3a, c3b, g0, g1, g2, g3, o_ref):
    for part in range(4):
        ks = slice(part * 256, part * 256 + 256)
        last = c3a[:, ks] if part < 2 else c3b[:, part * 256 - 512 : part * 256 - 256]
        total = dot(c0[:, ks], g0[...], 0, 0) + dot(c1[:, ks], g1[...], 0, 0)
        total += dot(c2[:, ks], g2[...], 0, 0) + dot(last, g3[...], 0, 0)
        o_ref[ks, :] = total.astype(BF)


def acts_kernel(s_ref, a_ref, *refs):
    o_ref = refs[-1]
    core = s_ref[0]
    half = a_ref.shape[1] // 2
    mine = a_ref[:, pl.ds(pl.multiple_of(core * half, 128), half)]
    other = a_ref[:, pl.ds(pl.multiple_of((1 - core) * half, 128), half)]
    row = 0
    for own, sent in zip(refs[:5], refs[5:10]):
        n = own.shape[0]
        total = dot(own[...], mine, 1, 1) + dot(sent[...], other, 1, 1)
        o_ref[row : row + n, :] = total.astype(BF)
        row += n


def seq_kernel(s_ref, ra, rb, rg, *o_refs):
    xh = s_ref[0]
    for s in range(2):
        near = rg[:, pl.ds(pl.multiple_of(xh * 256 + s * 128, 128), 128)]
        far = rg[:, pl.ds(pl.multiple_of((1 - xh) * 256 + s * 128, 128), 128)]
        cols = slice(s * 128, s * 128 + 128)
        right = jnp.concatenate([near, far], axis=1)
        for n in range(4):
            for dx in range(2):
                mine = ra[n * 160 + dx * 80 : n * 160 + dx * 80 + 80, cols]
                other = rb[n * 160 + 80 - dx * 80 : n * 160 + 160 - dx * 80, cols]
                left = jnp.concatenate([mine, other], axis=1)
                o_refs[n * 2 + dx][s] = dot(left, right, 1, 1).astype(BF)


def sum_kernel(s_ref, *refs):
    o_ref = refs[-1]
    xh = s_ref[0]
    for dx in range(2):
        total = sum(refs[n * 2 + dx][...].astype(F32) for n in range(4))
        place = jnp.where(dx == 0, xh, 1 - xh) * 512
        o_ref[:, :, pl.ds(pl.multiple_of(place, 128), 512)] = total.astype(BF)


def call(kernel, out, name, n_in, scalars=None):
    specs = [VMEM] * n_in
    if scalars is not None:
        specs = [SMEM] + specs
    many = isinstance(out, list)
    f = pl.pallas_call(
        kernel,
        out_shape=out,
        in_specs=specs,
        out_specs=[VMEM] * len(out) if many else VMEM,
        compiler_params=ROOM,
        name=name,
    )
    return f if scalars is None else lambda *a: f(scalars, *a)


def per_device(activations, out_grads, basis_in, basis_out, block_ids, seq_lens, query_grads):
    xl, core, xh, y = (lax.axis_index(a).astype(jnp.int32) for a in ("xl", "core", "xh", "y"))
    acts = lax.all_gather(activations, "z", axis=0, tiled=True)

    chosen, g0, g1, g2, g3 = pick(block_ids, y, basis_out, out_grads)
    g1, g2, g3 = shift(g1, y=1), shift(g2, y=-1), shift(g3, y=2)
    c1, c2 = shift(chosen, y=1), shift(chosen, y=-1)
    c3a, c3b = shift(c1[:, :512], y=1), shift(c2[:, 512:], y=-1)

    features = basis_in.shape[1]
    half = lax.dynamic_slice_in_dim(basis_in, core * (features // 2), features // 2, 1)
    own = jnp.concatenate([half, shift(half, xh=1)], axis=0)
    b1, b2 = shift(own, y=1), shift(own, y=-1)
    b3a, b3b = shift(b1[:80], y=1), shift(b2[80:], y=-1)
    bases = [own, b1, b2, b3a, b3b]
    bases += [shift(b, core=1) for b in bases]

    partial = call(grads_kernel, jax.ShapeDtypeStruct((1024, 512), BF), "grads", 9)(
        chosen, c1, c2, c3a, c3b, g0, g1, g2, g3
    )
    parts = lax.all_to_all(partial.reshape(16, 64, 512), ("xh", "z"), split_axis=0, concat_axis=0, tiled=True)
    summed = jnp.sum(parts.astype(F32), axis=0).astype(BF)
    col = lax.broadcasted_iota(jnp.int32, (1, 512), 1)
    pos = (col // 32 % 4) * 256 + col // 256 * 128 + y * 32 + col % 32
    limit = jnp.where(col % 256 < 128, seq_lens[0], seq_lens[1])
    rotated = jnp.where(pos < limit, summed, jnp.zeros((), BF))
    rotated_all = spread(rotated, "z", 8).reshape(512, 512)

    ra = call(acts_kernel, jax.ShapeDtypeStruct((640, 256), BF), "acts", 11, core[None])(acts, *bases)
    rb = shift(ra, xh=1)
    tiles = call(seq_kernel, [jax.ShapeDtypeStruct((2, 80, 512), BF)] * 8, "seq", 3, xh[None])(ra, rb, rotated_all)
    got = []
    for n, dy in enumerate((0, -1, 1, 2)):
        for dx in range(2):
            tile = tiles[n * 2 + dx]
            got.append(shift(tile, xh=dx, y=dy) if dx or dy else tile)
    seq_grads = call(sum_kernel, jax.ShapeDtypeStruct((2, 80, 1024), BF), "sums", 8, xh[None])(*got)

    sibling = shift(seq_grads, core=1)
    across = shift(seq_grads, xl=1)
    diagonal = shift(across, core=1)

    def score(grads):
        return jnp.einsum("sik,qik->sq", grads, query_grads, preferred_element_type=F32)

    pieces = jnp.stack([score(seq_grads), score(sibling), score(across), score(diagonal)])
    here = xl * 2 + core
    scores = jnp.concatenate(
        [lax.dynamic_index_in_dim(pieces, here ^ d, 0, keepdims=False) for d in range(4)], axis=0
    )
    scores = jnp.sum(spread(scores, ("xh", "y"), 8), axis=0)
    return jnp.sum(spread(scores, "z", 8), axis=0)


def solution(mesh):
    fine = Mesh(mesh.devices.reshape(2, 2, 8, 2, 4), ("xl", "core", "z", "xh", "y"))
    dp, eig = ("xl", "core"), ("z", "xh", "y")
    in_specs = (
        P(dp + eig, None),
        P(eig, dp),
        P(eig, None),
        P(eig, None),
        P(),
        P(dp),
        P(dp, eig, None),
    )
    return jax.shard_map(
        per_device, mesh=fine, in_specs=in_specs, out_specs=P(None, dp), check_vma=False
    )
```

```python
import jax
import jax.numpy as jnp
from jax import lax
from jax.experimental import pallas as pl
from jax.experimental.pallas import tpu as pltpu
from jax.sharding import Mesh, PartitionSpec as P

BLOCK = 128
LEN = 1024
BF = jnp.bfloat16
F32 = jnp.float32
SIZES = {"xl": 2, "core": 2, "z": 8, "xh": 2, "y": 4}
ROWS = (0, -1, 1, 2)
VMEM = pl.BlockSpec(memory_space=pltpu.VMEM)
SMEM = pl.BlockSpec(memory_space=pltpu.SMEM)
ROOM = pltpu.CompilerParams(vmem_limit_bytes=20 * 1024 * 1024)


def shift(x, **by):
    axes = tuple(by)
    count = 1
    for a in axes:
        count *= SIZES[a]
    pairs = []
    for source in range(count):
        rest, target, scale = source, 0, 1
        for a in reversed(axes):
            target += (rest % SIZES[a] + by[a]) % SIZES[a] * scale
            rest //= SIZES[a]
            scale *= SIZES[a]
        pairs.append((source, target))
    return lax.ppermute(x, axes, pairs)


def spread(x, axes, count):
    return lax.all_to_all(
        jnp.broadcast_to(x[None], (count,) + x.shape), axes, split_axis=0, concat_axis=0, tiled=True
    )


def dot(a, b, ca, cb):
    return lax.dot_general(a, b, (((ca,), (cb,)), ((), ())), preferred_element_type=F32)


def reorder(y, g_ref, outs):
    lane = lax.broadcasted_iota(jnp.int32, (1, 128), 1) // 32
    for xh in range(2):
        for part in range(2):
            start = part * 1024 + xh * 128
            cols = [g_ref[:, start + j * 256 : start + j * 256 + 128].astype(F32) for j in range(4)]
            place = xh * 256 + part * 128
            for o_ref, off, dy in outs:
                total = None
                for j in range(4):
                    moved = pltpu.roll(cols[j], ((j - dy - y + 8) % 4) * 32, 1)
                    total = moved if total is None else jnp.where(lane == j, moved, total)
                o_ref[:, off + place : off + place + 128] = total.astype(BF)


def pick_kernel(s_ref, *refs):
    picked, g_ref, up, down = refs[:8], *refs[8:]
    for n, p in enumerate(picked):
        cols = slice(n * 128, n * 128 + 128)
        up[:, cols] = p[...]
        down[:, cols] = p[...]
    reorder(s_ref[8], g_ref, ((up, 1024, 1), (down, 1024, -1)))


def pick(block_ids, y, basis_out, out_grads):
    rows, tokens = out_grads.shape
    whole = lambda width: pl.BlockSpec((rows, width), lambda g, s: (0, 0))
    spec = pltpu.PrefetchScalarGridSpec(
        num_scalar_prefetch=1,
        grid=(1,),
        in_specs=[pl.BlockSpec((rows, BLOCK), lambda g, s, n=n: (0, s[n])) for n in range(8)] + [whole(tokens)],
        out_specs=[whole(1536), whole(1536)],
    )
    return pl.pallas_call(
        pick_kernel,
        grid_spec=spec,
        out_shape=[arr(rows, 1536), arr(rows, 1536)],
        compiler_params=pltpu.CompilerParams(vmem_limit_bytes=52 * 1024 * 1024),
        name="pick",
    )(jnp.concatenate([block_ids, y[None]]), *[basis_out] * 8, out_grads)


def rest_kernel(y_ref, g_ref, aside, g0, g3):
    reorder(y_ref[0], g_ref, ((g3, 0, 2), (g0, 0, 0)))


def join_kernel(b0, b1, b2, aside, o_ref):
    o_ref[:80, :] = b0[...]
    o_ref[80:160, :] = b1[...]
    o_ref[160:, :] = b2[...]


def grads_kernel(here, up, down, c3, g0, g3, *refs):
    o_ref = refs[-1]
    for part in range(4):
        ks = slice(part * 256, part * 256 + 256)
        total = dot(here[:, ks], g0[...], 0, 0) + dot(c3[:, ks], g3[...], 0, 0)
        total += dot(up[:, ks], up[:, 1024:], 0, 0) + dot(down[:, ks], down[:, 1024:], 0, 0)
        o_ref[ks, :] = total.astype(BF)


def live_kernel(y_ref, lens, parts, *refs):
    o_ref = refs[-1]
    total = parts[0].astype(F32)
    for n in range(1, 16):
        total += parts[n].astype(F32)
    col = lax.broadcasted_iota(jnp.int32, (1, 512), 1)
    pos = (col // 32 % 4) * 256 + col // 256 * 128 + y_ref[0] * 32 + col % 32
    limit = jnp.where(col % 256 < 128, lens[0], lens[1])
    total = jnp.where(pos < limit, total, 0.0).astype(BF)
    for n in range(8):
        o_ref[n] = total


def acts_kernel(s_ref, a_ref, *refs):
    o_ref = refs[-1]
    core = s_ref[0]
    half = a_ref.shape[1] // 2
    mine = a_ref[:, pl.ds(pl.multiple_of(core * half, 128), half)]
    other = a_ref[:, pl.ds(pl.multiple_of((1 - core) * half, 128), half)]
    for n, (own, sent) in enumerate(zip(refs[:4], refs[4:8])):
        total = (dot(own[...], mine, 1, 1) + dot(sent[...], other, 1, 1)).astype(BF)
        for row in range(total.shape[0] // 80):
            place = (row + n // 2 * 3) * 160 + n % 2 * 80
            o_ref[place : place + 80, :] = total[row * 80 : row * 80 + 80]


def seq_kernel(xh_ref, y_ref, ra, rb, rg, o_ref):
    xh = xh_ref[0]
    for s in range(2):
        near = rg[:, pl.ds(pl.multiple_of(xh * 256 + s * 128, 128), 128)]
        far = rg[:, pl.ds(pl.multiple_of((1 - xh) * 256 + s * 128, 128), 128)]
        cols = slice(s * 128, s * 128 + 128)
        right = jnp.concatenate([near, far], axis=1)
        for n, dy in enumerate(ROWS):
            for dx in range(2):
                mine = ra[n * 160 + dx * 80 : n * 160 + dx * 80 + 80, cols]
                other = rb[n * 160 + 80 - dx * 80 : n * 160 + 160 - dx * 80, cols]
                left = jnp.concatenate([mine, other], axis=1)
                target = (xh + dx) % 2 * 4 + (y_ref[0] + dy + 4) % 4
                o_ref[target, s] = dot(left, right, 1, 1).astype(BF)


def sum_kernel(parts, o_ref):
    for xh in range(2):
        total = parts[xh * 4].astype(F32)
        for y in range(1, 4):
            total += parts[xh * 4 + y].astype(F32)
        o_ref[:, :, xh * 512 : xh * 512 + 512] = total.astype(BF)


def call(kernel, out, name, args, scalars=(), aside=()):
    specs = [SMEM] * len(scalars) + [VMEM] * len(args) + [pl.BlockSpec(memory_space=pltpu.HBM)] * len(aside)
    return pl.pallas_call(
        kernel,
        out_shape=out,
        in_specs=specs,
        out_specs=jax.tree.map(lambda _: VMEM, out),
        compiler_params=ROOM,
        name=name,
    )(*scalars, *args, *aside)


def arr(*shape):
    return jax.ShapeDtypeStruct(shape, BF)


def per_device(activations, out_grads, basis_in, basis_out, block_ids, seq_lens, query_grads):
    xl, core, xh, y = (lax.axis_index(a).astype(jnp.int32) for a in ("xl", "core", "xh", "y"))
    acts = lax.all_gather(activations, "z", axis=0, tiled=True)

    features = basis_in.shape[1]
    b0 = lax.dynamic_slice_in_dim(basis_in, core * (features // 2), features // 2, 1)
    b1, b2 = shift(b0, y=1), shift(b0, y=-1)
    up, down = pick(block_ids, y, basis_out, out_grads)
    g0, g3 = call(rest_kernel, [arr(216, 512)] * 2, "rest", [out_grads], [y[None]], [up])
    up_got, down_got, g3_got = shift(up, y=1), shift(down, y=-1), shift(g3, y=2)
    c3 = shift(down_got[:, :1024], y=-1)

    near = call(join_kernel, arr(240, features // 2), "join", [b0, b1, b2], (), [g0])
    far = shift(near, xh=1)
    near3 = shift(b1, y=1)
    far3 = shift(near3, xh=1)

    grads_in = [up, up_got, down_got, c3, g0, g3_got]
    partial = call(grads_kernel, arr(1024, 512), "grads", grads_in, (), [far, near3])
    parts = lax.all_to_all(partial.reshape(16, 64, 512), ("xh", "z"), split_axis=0, concat_axis=0, tiled=True)
    pieces = [near, far, near3, far3]
    others = [shift(b, core=1) for b in pieces]
    ra = call(acts_kernel, arr(640, 256), "acts", [acts] + pieces + others, [core[None]])
    copies = call(live_kernel, arr(8, 64, 512), "live", [parts], [y[None], seq_lens], [ra])
    rotated = lax.all_to_all(copies, "z", split_axis=0, concat_axis=0, tiled=True).reshape(512, 512)

    rb = shift(ra, xh=1)
    tiles = call(seq_kernel, arr(8, 2, 80, 512), "seq", [ra, rb, rotated], [xh[None], y[None]])
    got = lax.all_to_all(tiles, ("xh", "y"), split_axis=0, concat_axis=0, tiled=True)
    seq_grads = call(sum_kernel, arr(2, 80, 1024), "sums", [got])

    sibling = shift(seq_grads, core=1)
    across = shift(seq_grads, xl=1)
    diagonal = shift(across, core=1)

    def score(grads):
        return jnp.einsum("sik,qik->sq", grads, query_grads, preferred_element_type=F32)

    scored = jnp.stack([score(seq_grads), score(sibling), score(across), score(diagonal)])
    here = xl * 2 + core
    scores = jnp.concatenate(
        [lax.dynamic_index_in_dim(scored, here ^ d, 0, keepdims=False) for d in range(4)], axis=0
    )
    return jnp.sum(spread(scores, ("z", "xh", "y"), 64), axis=0)


def solution(mesh):
    fine = Mesh(mesh.devices.reshape(2, 2, 8, 2, 4), ("xl", "core", "z", "xh", "y"))
    dp, eig = ("xl", "core"), ("z", "xh", "y")
    in_specs = (
        P(dp + eig, None),
        P(eig, dp),
        P(eig, None),
        P(eig, None),
        P(),
        P(dp),
        P(dp, eig, None),
    )
    return jax.shard_map(
        per_device, mesh=fine, in_specs=in_specs, out_specs=P(None, dp), check_vma=False
    )
```

```python
import jax
import jax.numpy as jnp
from jax import lax
from jax.experimental import pallas as pl
from jax.experimental.pallas import tpu as pltpu
from jax.sharding import Mesh, PartitionSpec as P

BLOCK = 128
LEN = 1024
BF = jnp.bfloat16
F32 = jnp.float32
SIZES = {"xl": 2, "core": 2, "z": 8, "xh": 2, "y": 4}
ROWS = (0, -1, 1, 2)
VMEM = pl.BlockSpec(memory_space=pltpu.VMEM)
SMEM = pl.BlockSpec(memory_space=pltpu.SMEM)
WIDE = pltpu.CompilerParams(vmem_limit_bytes=52 * 1024 * 1024)
ROOM = pltpu.CompilerParams(vmem_limit_bytes=10 * 1024 * 1024)


def shift(x, **by):
    axes = tuple(by)
    count = 1
    for a in axes:
        count *= SIZES[a]
    pairs = []
    for source in range(count):
        rest, target, scale = source, 0, 1
        for a in reversed(axes):
            target += (rest % SIZES[a] + by[a]) % SIZES[a] * scale
            rest //= SIZES[a]
            scale *= SIZES[a]
        pairs.append((source, target))
    return lax.ppermute(x, axes, pairs)


def spread(x, axes, count):
    return lax.all_to_all(
        jnp.broadcast_to(x[None], (count,) + x.shape), axes, split_axis=0, concat_axis=0, tiled=True
    )


def dot(a, b, ca, cb):
    return lax.dot_general(a, b, (((ca,), (cb,)), ((), ())), preferred_element_type=F32)


def reorder(y, g_ref, outs):
    lane = lax.broadcasted_iota(jnp.int32, (1, 128), 1) // 32
    for xh in range(2):
        for part in range(2):
            start = part * 1024 + xh * 128
            cols = [g_ref[:, start + j * 256 : start + j * 256 + 128].astype(F32) for j in range(4)]
            place = xh * 256 + part * 128
            for o_ref, off, dy in outs:
                total = None
                for j in range(4):
                    moved = pltpu.roll(cols[j], ((j - dy - y + 8) % 4) * 32, 1)
                    total = moved if total is None else jnp.where(lane == j, moved, total)
                o_ref[:, off + place : off + place + 128] = total.astype(BF)


def pick_kernel(s_ref, *refs):
    picked, g_ref, up, down = refs[:8], *refs[8:]
    for n, p in enumerate(picked):
        cols = slice(n * 128, n * 128 + 128)
        up[:, cols] = p[...]
        down[:, cols] = p[...]
    reorder(s_ref[8], g_ref, ((up, 1024, 1), (down, 1024, -1)))


def pick(block_ids, y, basis_out, out_grads):
    rows, tokens = out_grads.shape
    whole = lambda width: pl.BlockSpec((rows, width), lambda g, s: (0, 0))
    spec = pltpu.PrefetchScalarGridSpec(
        num_scalar_prefetch=1,
        grid=(1,),
        in_specs=[pl.BlockSpec((rows, BLOCK), lambda g, s, n=n: (0, s[n])) for n in range(8)] + [whole(tokens)],
        out_specs=[whole(1536), whole(1536)],
    )
    return pl.pallas_call(
        pick_kernel,
        grid_spec=spec,
        out_shape=[arr(rows, 1536), arr(rows, 1536)],
        compiler_params=WIDE,
        name="pick",
    )(jnp.concatenate([block_ids, y[None]]), *[basis_out] * 8, out_grads)


def rest_kernel(y_ref, g_ref, aside, g0, g3):
    reorder(y_ref[0], g_ref, ((g3, 0, 2), (g0, 0, 0)))


def grads_kernel(here, up, down, c3, g0, g3, *refs):
    o_ref = refs[-1]
    for part in range(4):
        ks = slice(part * 256, part * 256 + 256)
        total = dot(here[:, ks], g0[...], 0, 0) + dot(c3[:, ks], g3[...], 0, 0)
        total += dot(up[:, ks], up[:, 1024:], 0, 0) + dot(down[:, ks], down[:, 1024:], 0, 0)
        o_ref[ks, :] = total.astype(BF)


def live_kernel(y_ref, lens, parts, *refs):
    o_ref = refs[-1]
    total = parts[0].astype(F32)
    for n in range(1, 16):
        total += parts[n].astype(F32)
    col = lax.broadcasted_iota(jnp.int32, (1, 512), 1)
    pos = (col // 32 % 4) * 256 + col // 256 * 128 + y_ref[0] * 32 + col % 32
    limit = jnp.where(col % 256 < 128, lens[0], lens[1])
    total = jnp.where(pos < limit, total, 0.0).astype(BF)
    for n in range(8):
        o_ref[n] = total


def acts_kernel(core_ref, a_ref, *refs):
    keep, send = refs[-2:]
    core = core_ref[0]
    for xh in range(2):
        cols = slice(xh * 256, xh * 256 + 256)
        for out, which in ((keep, core), (send, 1 - core)):
            tokens = a_ref[:, xh * 2 + which].reshape(256, a_ref.shape[3])
            for n in range(4):
                out[n * 160 : n * 160 + 160, cols] = dot(refs[n][...], tokens, 1, 1).astype(out.dtype)


def add_kernel(a, b, keep, send):
    total = a[...] + b[...].astype(F32)
    keep[...] = total
    send[...] = total.astype(BF)


def seq_kernel(xh_ref, y_ref, ra, rb, rg, o_ref):
    xh = xh_ref[0]
    for s in range(2):
        near, far = slice(s * 128, s * 128 + 128), slice(s * 128 + 256, s * 128 + 384)
        right = jnp.concatenate([rg[:, near], rg[:, far]], axis=1)
        for n, dy in enumerate(ROWS):
            for dx in range(2):
                mine = slice(n * 160 + dx * 80, n * 160 + dx * 80 + 80)
                other = slice(n * 160 + 80 - dx * 80, n * 160 + 160 - dx * 80)
                left = [ra[mine, cols] + rb[other, cols].astype(F32) for cols in (near, far)]
                left = jnp.concatenate(left, axis=1).astype(BF)
                target = (xh + dx) % 2 * 4 + (y_ref[0] + dy + 4) % 4
                o_ref[target, s] = dot(left, right, 1, 1).astype(BF)


def sum_kernel(parts, o_ref):
    for xh in range(2):
        total = parts[xh * 4].astype(F32)
        for y in range(1, 4):
            total += parts[xh * 4 + y].astype(F32)
        o_ref[:, :, xh * 512 : xh * 512 + 512] = total.astype(BF)


def call(kernel, out, name, args, scalars=(), aside=()):
    specs = [SMEM] * len(scalars) + [VMEM] * len(args) + [pl.BlockSpec(memory_space=pl.ANY)] * len(aside)
    return pl.pallas_call(
        kernel,
        out_shape=out,
        in_specs=specs,
        out_specs=jax.tree.map(lambda _: VMEM, out),
        compiler_params=ROOM,
        name=name,
    )(*scalars, *args, *aside)


def arr(*shape):
    return jax.ShapeDtypeStruct(shape, BF)


def per_device(activations, out_grads, basis_in, basis_out, block_ids, seq_lens, query_grads):
    xl, core, xh, y = (lax.axis_index(a).astype(jnp.int32) for a in ("xl", "core", "xh", "y"))
    slots, features = activations.shape
    part = features // 4
    acts = activations.reshape(slots, 4, part).transpose(1, 0, 2)
    acts = lax.all_to_all(acts, ("xh", "core"), split_axis=0, concat_axis=0, tiled=True)
    acts = lax.all_gather(acts, "z", axis=0, tiled=False)

    def quarter(x):
        return lax.dynamic_slice_in_dim(basis_in, (x * 2 + core) * part, part, 1)

    b0 = jnp.concatenate([quarter(xh), shift(quarter(1 - xh), xh=1)])
    b1, b2 = shift(b0, y=1), shift(b0, y=-1)
    b3 = shift(b1, y=1)

    up, down = pick(block_ids, y, basis_out, out_grads)
    g0, g3 = call(rest_kernel, [arr(216, 512)] * 2, "rest", [out_grads], [y[None]], [up])
    up_got, down_got, g3_got = shift(up, y=1), shift(down, y=-1), shift(g3, y=2)
    c3 = shift(down_got[:, :1024], y=-1)

    grads_in = [up, up_got, down_got, c3, g0, g3_got]
    partial = call(grads_kernel, arr(1024, 512), "grads", grads_in, (), [b2, b3])
    parts = lax.all_to_all(partial.reshape(16, 64, 512), ("xh", "z"), split_axis=0, concat_axis=0, tiled=True)
    sums = [jax.ShapeDtypeStruct((640, 512), F32), arr(640, 512)]
    keep, send = call(acts_kernel, sums, "acts", [acts, b0, b1, b2, b3], [core[None]])
    keep, send = call(add_kernel, sums, "add", [keep, shift(send, core=1)])
    rb = shift(send, xh=1)
    copies = call(live_kernel, arr(8, 64, 512), "live", [parts], [y[None], seq_lens], [send])
    rotated = lax.all_to_all(copies, "z", split_axis=0, concat_axis=0, tiled=True).reshape(512, 512)

    tiles = call(seq_kernel, arr(8, 2, 80, 512), "seq", [keep, rb, rotated], [xh[None], y[None]])
    got = lax.all_to_all(tiles, ("xh", "y"), split_axis=0, concat_axis=0, tiled=True)
    seq_grads = call(sum_kernel, arr(2, 80, 1024), "sums", [got])

    sibling = shift(seq_grads, core=1)
    across = shift(seq_grads, xl=1)
    diagonal = shift(across, core=1)

    def score(grads):
        return jnp.einsum("sik,qik->sq", grads, query_grads, preferred_element_type=F32)

    scored = jnp.stack([score(seq_grads), score(sibling), score(across), score(diagonal)])
    here = xl * 2 + core
    scores = jnp.concatenate(
        [lax.dynamic_index_in_dim(scored, here ^ d, 0, keepdims=False) for d in range(4)], axis=0
    )
    return jnp.sum(spread(scores, ("z", "xh", "y"), 64), axis=0)


def solution(mesh):
    fine = Mesh(mesh.devices.reshape(2, 2, 8, 2, 4), ("xl", "core", "z", "xh", "y"))
    dp, eig = ("xl", "core"), ("z", "xh", "y")
    in_specs = (
        P(dp + eig, None),
        P(eig, dp),
        P(eig, None),
        P(eig, None),
        P(),
        P(dp),
        P(dp, eig, None),
    )
    return jax.shard_map(
        per_device, mesh=fine, in_specs=in_specs, out_specs=P(None, dp), check_vma=False
    )
```

```python
import jax
import jax.numpy as jnp
from jax import lax
from jax.experimental import pallas as pl
from jax.experimental.pallas import tpu as pltpu
from jax.sharding import Mesh, PartitionSpec as P

BLOCK = 128
LEN = 1024
BF = jnp.bfloat16
F32 = jnp.float32
SIZES = {"xl": 2, "core": 2, "z": 8, "xh": 2, "y": 4}
ROWS = (0, -1, 1, 2)
VMEM = pl.BlockSpec(memory_space=pltpu.VMEM)
SMEM = pl.BlockSpec(memory_space=pltpu.SMEM)
WIDE = pltpu.CompilerParams(vmem_limit_bytes=52 * 1024 * 1024)
ROOM = pltpu.CompilerParams(vmem_limit_bytes=10 * 1024 * 1024)


def shift(x, **by):
    axes = tuple(by)
    count = 1
    for a in axes:
        count *= SIZES[a]
    pairs = []
    for source in range(count):
        rest, target, scale = source, 0, 1
        for a in reversed(axes):
            target += (rest % SIZES[a] + by[a]) % SIZES[a] * scale
            rest //= SIZES[a]
            scale *= SIZES[a]
        pairs.append((source, target))
    return lax.ppermute(x, axes, pairs)


def spread(x, axes, count):
    return lax.all_to_all(
        jnp.broadcast_to(x[None], (count,) + x.shape), axes, split_axis=0, concat_axis=0, tiled=True
    )


def dot(a, b, ca, cb):
    return lax.dot_general(a, b, (((ca,), (cb,)), ((), ())), preferred_element_type=F32)


def reorder(y, g_ref, outs):
    lane = lax.broadcasted_iota(jnp.int32, (1, 128), 1) // 32
    for xh in range(2):
        for part in range(2):
            start = part * 1024 + xh * 128
            cols = [g_ref[:, start + j * 256 : start + j * 256 + 128].astype(F32) for j in range(4)]
            place = xh * 256 + part * 128
            for o_ref, off, dy in outs:
                total = None
                for j in range(4):
                    moved = pltpu.roll(cols[j], ((j - dy - y + 8) % 4) * 32, 1)
                    total = moved if total is None else jnp.where(lane == j, moved, total)
                o_ref[:, off + place : off + place + 128] = total.astype(BF)


def pick_kernel(s_ref, *refs):
    picked, g_ref, up, down, g0, g3 = refs[:8], *refs[8:]
    for n, p in enumerate(picked):
        cols = slice(n * 128, n * 128 + 128)
        up[:, cols] = p[...]
        down[:, cols] = p[...]
    reorder(s_ref[8], g_ref, ((up, 1024, 1), (down, 1024, -1), (g3, 0, 2), (g0, 0, 0)))


def pick(block_ids, y, basis_out, out_grads):
    rows, tokens = out_grads.shape
    whole = lambda width: pl.BlockSpec((rows, width), lambda g, s: (0, 0))
    spec = pltpu.PrefetchScalarGridSpec(
        num_scalar_prefetch=1,
        grid=(1,),
        in_specs=[pl.BlockSpec((rows, BLOCK), lambda g, s, n=n: (0, s[n])) for n in range(8)] + [whole(tokens)],
        out_specs=[whole(1536), whole(1536), whole(512), whole(512)],
    )
    return pl.pallas_call(
        pick_kernel,
        grid_spec=spec,
        out_shape=[arr(rows, 1536), arr(rows, 1536), arr(rows, 512), arr(rows, 512)],
        compiler_params=WIDE,
        name="pick",
    )(jnp.concatenate([block_ids, y[None]]), *[basis_out] * 8, out_grads)


def cut_kernel(xh_ref, core_ref, a_ref, b_ref, a_own, a_sib, b_own):
    part = a_ref.shape[1] // 4
    for near in range(2):
        x = (xh_ref[0] + near) % 2
        mine = pl.ds(pl.multiple_of((x * 2 + core_ref[0]) * part, 128), part)
        other = pl.ds(pl.multiple_of((x * 2 + 1 - core_ref[0]) * part, 128), part)
        cols = slice(near * part, near * part + part)
        a_own[:, cols] = a_ref[:, mine]
        a_sib[:, cols] = a_ref[:, other]
        b_own[:, cols] = b_ref[:, mine]


def pair_kernel(own, sib, aside, near, far):
    part = near.shape[2]
    for n, a in enumerate((own, sib)):
        near[n] = a[:, :part]
        far[n] = a[:, part:]


def stack_kernel(near, far, *refs):
    o_ref = refs[-1]
    o_ref[:2] = near[...]
    o_ref[2:] = far[...]


def join_kernel(b0, b1, b2, aside, o_ref):
    part = b0.shape[1] // 2
    for n, b in enumerate((b0, b1, b2)):
        o_ref[n * 80 : n * 80 + 80, :] = b[:, part:]


def grads_kernel(here, up, down, c3, g0, g3, *refs):
    o_ref = refs[-1]
    for part in range(4):
        ks = slice(part * 256, part * 256 + 256)
        total = dot(here[:, ks], g0[...], 0, 0) + dot(c3[:, ks], g3[...], 0, 0)
        total += dot(up[:, ks], up[:, 1024:], 0, 0) + dot(down[:, ks], down[:, 1024:], 0, 0)
        o_ref[ks, :] = total.astype(BF)


def live_kernel(y_ref, lens, parts, *refs):
    o_ref = refs[-1]
    total = parts[0].astype(F32)
    for n in range(1, 16):
        total += parts[n].astype(F32)
    col = lax.broadcasted_iota(jnp.int32, (1, 512), 1)
    pos = (col // 32 % 4) * 256 + col // 256 * 128 + y_ref[0] * 32 + col % 32
    limit = jnp.where(col % 256 < 128, lens[0], lens[1])
    total = jnp.where(pos < limit, total, 0.0).astype(BF)
    for n in range(8):
        o_ref[n] = total


def acts_kernel(xh_ref, a_ref, b0, b1, b2, b3, far, far3, keep, send):
    part = a_ref.shape[3]
    rows = [(n * 160, b, slice(0, 80), slice(0, part)) for n, b in enumerate((b0, b1, b2, b3))]
    rows += [(n * 160 + 80, far, slice(n * 80, n * 80 + 80), slice(0, part)) for n in range(3)]
    rows += [(560, far3, slice(0, 80), slice(0, part))]
    for xh in range(2):
        cols = slice(xh * 256, xh * 256 + 256)
        for core, out in enumerate((keep, send)):
            tokens = a_ref[:, (xh_ref[0] + xh) % 2 * 2 + core].reshape(256, part)
            for place, b, r, c in rows:
                out[place : place + 80, cols] = dot(b[r, c], tokens, 1, 1)


def add_kernel(a, b, keep, send):
    total = a[...] + b[...]
    keep[...] = total
    send[...] = total.astype(BF)


def seq_kernel(xh_ref, y_ref, ra, rb, rg, o_ref):
    xh = xh_ref[0]
    for s in range(2):
        near, far = slice(s * 128, s * 128 + 128), slice(s * 128 + 256, s * 128 + 384)
        right = jnp.concatenate([rg[:, near], rg[:, far]], axis=1)
        for n, dy in enumerate(ROWS):
            for dx in range(2):
                mine = slice(n * 160 + dx * 80, n * 160 + dx * 80 + 80)
                other = slice(n * 160 + 80 - dx * 80, n * 160 + 160 - dx * 80)
                left = [ra[mine, cols] + rb[other, cols].astype(F32) for cols in (near, far)]
                left = jnp.concatenate(left, axis=1).astype(BF)
                target = (xh + dx) % 2 * 4 + (y_ref[0] + dy + 4) % 4
                o_ref[target, s] = dot(left, right, 1, 1).astype(BF)


def sum_kernel(parts, o_ref):
    for xh in range(2):
        total = parts[xh * 4].astype(F32)
        for y in range(1, 4):
            total += parts[xh * 4 + y].astype(F32)
        o_ref[:, :, xh * 512 : xh * 512 + 512] = total.astype(BF)


def call(kernel, out, name, args, scalars=(), aside=()):
    specs = [SMEM] * len(scalars) + [VMEM] * len(args) + [pl.BlockSpec(memory_space=pl.ANY)] * len(aside)
    return pl.pallas_call(
        kernel,
        out_shape=out,
        in_specs=specs,
        out_specs=jax.tree.map(lambda _: VMEM, out),
        compiler_params=WIDE if name in ("acts", "seq") else ROOM,
        name=name,
    )(*scalars, *args, *aside)


def arr(*shape):
    return jax.ShapeDtypeStruct(shape, BF)


def per_device(activations, out_grads, basis_in, basis_out, block_ids, seq_lens, query_grads):
    xl, core, xh, y = (lax.axis_index(a).astype(jnp.int32) for a in ("xl", "core", "xh", "y"))
    slots, features = activations.shape
    part = features // 4
    place = [xh[None], core[None]]
    cuts = [arr(slots, 2 * part), arr(slots, 2 * part), arr(80, 2 * part)]
    a_own, a_sib, b0 = call(cut_kernel, cuts, "cut", [activations, basis_in], place)
    b1, b2 = shift(b0, y=1), shift(b0, y=-1)
    a_sib = shift(a_sib, core=1)
    up, down, g0, g3 = pick(block_ids, y, basis_out, out_grads)
    near, a_far = call(pair_kernel, [arr(2, slots, part)] * 2, "pair", [a_own, a_sib], (), [g0])
    a_far = shift(a_far, xh=1)
    up_got, down_got, g3_got = shift(up, y=1), shift(down, y=-1), shift(g3, y=2)
    acts = call(stack_kernel, arr(4, slots, part), "stack", [near, a_far], (), [down_got, up_got, b1, b2])
    acts = lax.all_gather(acts, "z", axis=0, tiled=False)
    c3 = shift(down_got[:, :1024], y=-1)
    b3 = shift(b1, y=1)
    far = shift(call(join_kernel, arr(240, part), "join", [b0, b1, b2], (), [g0]), xh=1)
    far3 = shift(b3[:, part:], xh=1)

    grads_in = [up, up_got, down_got, c3, g0, g3_got]
    partial = call(grads_kernel, arr(1024, 512), "grads", grads_in, (), [far, b3])
    parts = lax.all_to_all(partial.reshape(16, 64, 512), ("xh", "z"), split_axis=0, concat_axis=0, tiled=True)
    wide = jax.ShapeDtypeStruct((640, 512), F32)
    keep, send = call(acts_kernel, [wide, wide], "acts", [acts, b0, b1, b2, b3, far, far3], [xh[None]])
    keep, send = call(add_kernel, [wide, arr(640, 512)], "add", [keep, shift(send, core=1)])
    rb = shift(send, xh=1)
    copies = call(live_kernel, arr(8, 64, 512), "live", [parts], [y[None], seq_lens], [send])
    rotated = lax.all_to_all(copies, "z", split_axis=0, concat_axis=0, tiled=True).reshape(512, 512)

    tiles = call(seq_kernel, arr(8, 2, 80, 512), "seq", [keep, rb, rotated], [xh[None], y[None]])
    got = lax.all_to_all(tiles, ("xh", "y"), split_axis=0, concat_axis=0, tiled=True)
    seq_grads = call(sum_kernel, arr(2, 80, 1024), "sums", [got])

    sibling = shift(seq_grads, core=1)
    across = shift(seq_grads, xl=1)
    diagonal = shift(across, core=1)

    def score(grads):
        return jnp.einsum("sik,qik->sq", grads, query_grads, preferred_element_type=F32)

    scored = jnp.stack([score(seq_grads), score(sibling), score(across), score(diagonal)])
    here = xl * 2 + core
    scores = jnp.concatenate(
        [lax.dynamic_index_in_dim(scored, here ^ d, 0, keepdims=False) for d in range(4)], axis=0
    )
    return jnp.sum(spread(scores, ("z", "xh", "y"), 64), axis=0)


def solution(mesh):
    fine = Mesh(mesh.devices.reshape(2, 2, 8, 2, 4), ("xl", "core", "z", "xh", "y"))
    dp, eig = ("xl", "core"), ("z", "xh", "y")
    in_specs = (
        P(dp + eig, None),
        P(eig, dp),
        P(eig, None),
        P(eig, None),
        P(),
        P(dp),
        P(dp, eig, None),
    )
    return jax.shard_map(
        per_device, mesh=fine, in_specs=in_specs, out_specs=P(None, dp), check_vma=False
    )
```

```python
import jax
import jax.numpy as jnp
from jax import lax
from jax.experimental import pallas as pl
from jax.experimental.pallas import tpu as pltpu
from jax.sharding import Mesh, PartitionSpec as P

BLOCK = 128
LEN = 1024
BF = jnp.bfloat16
F32 = jnp.float32
SIZES = {"xl": 2, "core": 2, "z": 8, "xh": 2, "y": 4}
ROWS = (0, -1, 1, 2)
VMEM = pl.BlockSpec(memory_space=pltpu.VMEM)
SMEM = pl.BlockSpec(memory_space=pltpu.SMEM)
WIDE = pltpu.CompilerParams(vmem_limit_bytes=52 * 1024 * 1024)
ROOM = pltpu.CompilerParams(vmem_limit_bytes=10 * 1024 * 1024)


def shift(x, **by):
    axes = tuple(by)
    count = 1
    for a in axes:
        count *= SIZES[a]
    pairs = []
    for source in range(count):
        rest, target, scale = source, 0, 1
        for a in reversed(axes):
            target += (rest % SIZES[a] + by[a]) % SIZES[a] * scale
            rest //= SIZES[a]
            scale *= SIZES[a]
        pairs.append((source, target))
    return lax.ppermute(x, axes, pairs)


def spread(x, axes, count):
    return lax.all_to_all(
        jnp.broadcast_to(x[None], (count,) + x.shape), axes, split_axis=0, concat_axis=0, tiled=True
    )


def dot(a, b, ca, cb):
    return lax.dot_general(a, b, (((ca,), (cb,)), ((), ())), preferred_element_type=F32)


def reorder(y, g_ref, outs):
    lane = lax.broadcasted_iota(jnp.int32, (1, 128), 1) // 32
    for xh in range(2):
        for part in range(2):
            start = part * 1024 + xh * 128
            cols = [g_ref[:, start + j * 256 : start + j * 256 + 128].astype(F32) for j in range(4)]
            place = xh * 256 + part * 128
            for o_ref, off, dy in outs:
                total = None
                for j in range(4):
                    moved = pltpu.roll(cols[j], ((j - dy - y + 8) % 4) * 32, 1)
                    total = moved if total is None else jnp.where(lane == j, moved, total)
                o_ref[:, off + place : off + place + 128] = total.astype(BF)


def pick_kernel(s_ref, *refs):
    picked, g_ref, first, up, down, g0, g3 = refs[:8], *refs[8:]
    for n in range(4):
        cols = slice(n * 128, n * 128 + 128)
        first[:, cols] = picked[n][...]
        up[:, cols] = picked[n + 4][...]
        down[:, cols] = picked[n + 4][...]
    reorder(s_ref[8], g_ref, ((up, 512, 1), (down, 512, -1), (g3, 0, 2), (g0, 0, 0)))


def pick(block_ids, y, basis_out, out_grads):
    rows, tokens = out_grads.shape
    whole = lambda width: pl.BlockSpec((rows, width), lambda g, s: (0, 0))
    widths = (512, 1024, 1024, 512, 512)
    spec = pltpu.PrefetchScalarGridSpec(
        num_scalar_prefetch=1,
        grid=(1,),
        in_specs=[pl.BlockSpec((rows, BLOCK), lambda g, s, n=n: (0, s[n])) for n in range(8)] + [whole(tokens)],
        out_specs=[whole(w) for w in widths],
    )
    return pl.pallas_call(
        pick_kernel,
        grid_spec=spec,
        out_shape=[arr(rows, w) for w in widths],
        compiler_params=WIDE,
        name="pick",
    )(jnp.concatenate([block_ids, y[None]]), *[basis_out] * 8, out_grads)


def cut_kernel(xh_ref, core_ref, a_ref, b_ref, a_own, a_sib, b_own):
    part = a_ref.shape[1] // 4
    for near in range(2):
        x = (xh_ref[0] + near) % 2
        mine = pl.ds(pl.multiple_of((x * 2 + core_ref[0]) * part, 128), part)
        other = pl.ds(pl.multiple_of((x * 2 + 1 - core_ref[0]) * part, 128), part)
        cols = slice(near * part, near * part + part)
        a_own[:, cols] = a_ref[:, mine]
        a_sib[:, cols] = a_ref[:, other]
        b_own[:, cols] = b_ref[:, mine]


def pair_kernel(own, sib, b_own, aside, near, far):
    part = near.shape[2]
    for n, a in enumerate((own, sib)):
        near[n] = a[:, :part]
        far[n * 32 : n * 32 + 32, :] = a[:, part:]
    far[64:, :] = b_own[:, part:]


def stack_kernel(near, far, b_own, *refs):
    o_ref, b0 = refs[-2:]
    o_ref[:2] = near[...]
    o_ref[2] = far[:32, :]
    o_ref[3] = far[32:64, :]
    b0[:80, :] = b_own[:, : b0.shape[1]]
    b0[80:, :] = far[64:, :]


def grads_kernel(ca, mine, ca1, up, ca2, down, c3a, c3b, g0, g3, o_ref):
    for n, (c0, c1, c2, c3) in enumerate(((ca, ca1, ca2, c3a), (mine, up, down, c3b))):
        for place in (0, 256):
            ks = slice(place, place + 256)
            total = dot(c0[:, ks], g0[...], 0, 0) + dot(c3[:, ks], g3[...], 0, 0)
            total += dot(c1[:, ks], up[:, 512:], 0, 0) + dot(c2[:, ks], down[:, 512:], 0, 0)
            o_ref[n * 512 + place : n * 512 + place + 256, :] = total.astype(BF)


def live_kernel(y_ref, lens, parts, *refs):
    o_ref = refs[-1]
    total = parts[0].astype(F32)
    for n in range(1, 16):
        total += parts[n].astype(F32)
    col = lax.broadcasted_iota(jnp.int32, (1, 512), 1)
    pos = (col // 32 % 4) * 256 + col // 256 * 128 + y_ref[0] * 32 + col % 32
    limit = jnp.where(col % 256 < 128, lens[0], lens[1])
    total = jnp.where(pos < limit, total, 0.0).astype(BF)
    for n in range(8):
        o_ref[n] = total


def acts_kernel(xh_ref, a_ref, b0, b1, b2, b3, keep, send):
    part = a_ref.shape[3]
    for xh in range(2):
        cols = slice(xh * 256, xh * 256 + 256)
        for core, out in enumerate((keep, send)):
            tokens = a_ref[:, (xh_ref[0] + xh) % 2 * 2 + core].reshape(256, part)
            for n, b in enumerate((b0, b1, b2, b3)):
                out[n * 160 : n * 160 + 160, cols] = dot(b[...], tokens, 1, 1)


def add_kernel(a, b, keep, send):
    total = a[...] + b[...]
    keep[...] = total
    send[...] = total.astype(BF)


def seq_kernel(xh_ref, y_ref, ra, rb, rg, o_ref):
    xh = xh_ref[0]
    for s in range(2):
        near, far = slice(s * 128, s * 128 + 128), slice(s * 128 + 256, s * 128 + 384)
        right = jnp.concatenate([rg[:, near], rg[:, far]], axis=1)
        for n, dy in enumerate(ROWS):
            for dx in range(2):
                mine = slice(n * 160 + dx * 80, n * 160 + dx * 80 + 80)
                other = slice(n * 160 + 80 - dx * 80, n * 160 + 160 - dx * 80)
                left = [ra[mine, cols] + rb[other, cols].astype(F32) for cols in (near, far)]
                left = jnp.concatenate(left, axis=1).astype(BF)
                target = (xh + dx) % 2 * 4 + (y_ref[0] + dy + 4) % 4
                o_ref[target, s] = dot(left, right, 1, 1).astype(BF)


def sum_kernel(parts, o_ref):
    for xh in range(2):
        total = parts[xh * 4].astype(F32)
        for y in range(1, 4):
            total += parts[xh * 4 + y].astype(F32)
        o_ref[:, :, xh * 512 : xh * 512 + 512] = total.astype(BF)


def call(kernel, out, name, args, scalars=(), aside=()):
    specs = [SMEM] * len(scalars) + [VMEM] * len(args) + [pl.BlockSpec(memory_space=pl.ANY)] * len(aside)
    return pl.pallas_call(
        kernel,
        out_shape=out,
        in_specs=specs,
        out_specs=jax.tree.map(lambda _: VMEM, out),
        compiler_params=ROOM,
        name=name,
    )(*scalars, *args, *aside)


def arr(*shape):
    return jax.ShapeDtypeStruct(shape, BF)


def per_device(activations, out_grads, basis_in, basis_out, block_ids, seq_lens, query_grads):
    xl, core, xh, y = (lax.axis_index(a).astype(jnp.int32) for a in ("xl", "core", "xh", "y"))
    slots, features = activations.shape
    part = features // 4
    place = [xh[None], core[None]]
    cuts = [arr(slots, 2 * part), arr(slots, 2 * part), arr(80, 2 * part)]
    a_own, a_sib, b_own = call(cut_kernel, cuts, "cut", [activations, basis_in], place)
    a_sib = shift(a_sib, core=1)

    first, up, down, g0, g3 = pick(block_ids, y, basis_out, out_grads)
    first_up, first_down = shift(first, y=1), shift(first, y=-1)
    near, far = call(pair_kernel, [arr(2, slots, part), arr(144, part)], "pair", [a_own, a_sib, b_own], (), [g0])
    far = shift(far, xh=1)
    acts, b0 = call(
        stack_kernel, [arr(4, slots, part), arr(160, part)], "stack", [near, far, b_own], (), [first_up, first_down]
    )
    acts = lax.all_gather(acts, "z", axis=0, tiled=False)
    up_got, down_got, g3_got = shift(up, y=1), shift(down, y=-1), shift(g3, y=2)
    c3a = shift(first_down, y=-1)
    c3b = shift(down_got[:, :512], y=-1)

    grads_in = [first, up, first_up, up_got, first_down, down_got, c3a, c3b, g0, g3_got]
    partial = call(grads_kernel, arr(1024, 512), "grads", grads_in)
    b1, b2 = shift(b0, y=1), shift(b0, y=-1)
    b3 = shift(b1, y=1)
    parts = lax.all_to_all(partial.reshape(16, 64, 512), ("xh", "z"), split_axis=0, concat_axis=0, tiled=True)
    wide = jax.ShapeDtypeStruct((640, 512), F32)
    keep, send = call(acts_kernel, [wide, wide], "acts", [acts, b0, b1, b2, b3], [xh[None]])
    keep, send = call(add_kernel, [wide, arr(640, 512)], "add", [keep, shift(send, core=1)])
    rb = shift(send, xh=1)
    copies = call(live_kernel, arr(8, 64, 512), "live", [parts], [y[None], seq_lens], [send])
    rotated = lax.all_to_all(copies, "z", split_axis=0, concat_axis=0, tiled=True).reshape(512, 512)

    tiles = call(seq_kernel, arr(8, 2, 80, 512), "seq", [keep, rb, rotated], [xh[None], y[None]])
    got = lax.all_to_all(tiles, ("xh", "y"), split_axis=0, concat_axis=0, tiled=True)
    seq_grads = call(sum_kernel, arr(2, 80, 1024), "sums", [got])

    sibling = shift(seq_grads, core=1)
    across = shift(seq_grads, xl=1)
    diagonal = shift(across, core=1)

    def score(grads):
        return jnp.einsum("sik,qik->sq", grads, query_grads, preferred_element_type=F32)

    scored = jnp.stack([score(seq_grads), score(sibling), score(across), score(diagonal)])
    here = xl * 2 + core
    scores = jnp.concatenate(
        [lax.dynamic_index_in_dim(scored, here ^ d, 0, keepdims=False) for d in range(4)], axis=0
    )
    return jnp.sum(spread(scores, ("z", "xh", "y"), 64), axis=0)


def solution(mesh):
    fine = Mesh(mesh.devices.reshape(2, 2, 8, 2, 4), ("xl", "core", "z", "xh", "y"))
    dp, eig = ("xl", "core"), ("z", "xh", "y")
    in_specs = (
        P(dp + eig, None),
        P(eig, dp),
        P(eig, None),
        P(eig, None),
        P(),
        P(dp),
        P(dp, eig, None),
    )
    return jax.shard_map(
        per_device, mesh=fine, in_specs=in_specs, out_specs=P(None, dp), check_vma=False
    )
```

```python
import jax
import jax.numpy as jnp
from jax import lax
from jax.experimental import pallas as pl
from jax.experimental.pallas import tpu as pltpu
from jax.sharding import Mesh, PartitionSpec as P

BLOCK = 128
LEN = 1024
BF = jnp.bfloat16
F32 = jnp.float32
SIZES = {"xl": 2, "core": 2, "z": 8, "xh": 2, "y": 4}
ROWS = (0, -1, 1, 2)
VMEM = pl.BlockSpec(memory_space=pltpu.VMEM)
SMEM = pl.BlockSpec(memory_space=pltpu.SMEM)
WIDE = pltpu.CompilerParams(vmem_limit_bytes=52 * 1024 * 1024)
ROOM = pltpu.CompilerParams(vmem_limit_bytes=10 * 1024 * 1024)


def shift(x, **by):
    axes = tuple(by)
    count = 1
    for a in axes:
        count *= SIZES[a]
    pairs = []
    for source in range(count):
        rest, target, scale = source, 0, 1
        for a in reversed(axes):
            target += (rest % SIZES[a] + by[a]) % SIZES[a] * scale
            rest //= SIZES[a]
            scale *= SIZES[a]
        pairs.append((source, target))
    return lax.ppermute(x, axes, pairs)


def spread(x, axes, count):
    return lax.all_to_all(
        jnp.broadcast_to(x[None], (count,) + x.shape), axes, split_axis=0, concat_axis=0, tiled=True
    )


def dot(a, b, ca, cb):
    return lax.dot_general(a, b, (((ca,), (cb,)), ((), ())), preferred_element_type=F32)


def reorder(y, g_ref, outs):
    lane = lax.broadcasted_iota(jnp.int32, (1, 128), 1) // 32
    for xh in range(2):
        for part in range(2):
            start = part * 1024 + xh * 128
            cols = [g_ref[:, start + j * 256 : start + j * 256 + 128].astype(F32) for j in range(4)]
            place = xh * 256 + part * 128
            for o_ref, off, dy in outs:
                total = None
                for j in range(4):
                    moved = pltpu.roll(cols[j], ((j - dy - y + 8) % 4) * 32, 1)
                    total = moved if total is None else jnp.where(lane == j, moved, total)
                o_ref[:, off + place : off + place + 128] = total.astype(BF)


def pick_kernel(s_ref, *refs):
    picked, g_ref, chosen, g0, g1, g2, g3 = refs[:8], *refs[8:]
    for n, p in enumerate(picked):
        chosen[:, n * 128 : n * 128 + 128] = p[...]
    reorder(s_ref[8], g_ref, ((g1, 0, 1), (g2, 0, -1), (g3, 0, 2), (g0, 0, 0)))


def pick(block_ids, y, basis_out, out_grads):
    rows, tokens = out_grads.shape
    whole = lambda width: pl.BlockSpec((rows, width), lambda g, s: (0, 0))
    widths = (1024, 512, 512, 512, 512)
    spec = pltpu.PrefetchScalarGridSpec(
        num_scalar_prefetch=1,
        grid=(1,),
        in_specs=[pl.BlockSpec((rows, BLOCK), lambda g, s, n=n: (0, s[n])) for n in range(8)] + [whole(tokens)],
        out_specs=[whole(w) for w in widths],
    )
    return pl.pallas_call(
        pick_kernel,
        grid_spec=spec,
        out_shape=[arr(rows, w) for w in widths],
        compiler_params=WIDE,
        name="pick",
    )(jnp.concatenate([block_ids, y[None]]), *[basis_out] * 8, out_grads)


def cut_kernel(xh_ref, core_ref, a_ref, b_ref, aside, a_own, a_sib, b_own):
    part = a_ref.shape[1] // 4
    for near in range(2):
        x = (xh_ref[0] + near) % 2
        mine = pl.ds(pl.multiple_of((x * 2 + core_ref[0]) * part, 128), part)
        other = pl.ds(pl.multiple_of((x * 2 + 1 - core_ref[0]) * part, 128), part)
        cols = slice(near * part, near * part + part)
        a_own[:, cols] = a_ref[:, mine]
        a_sib[:, cols] = a_ref[:, other]
        b_own[:, cols] = b_ref[:, mine]


def pair_kernel(own, sib, b_own, aside, near, far, b_far):
    part = near.shape[2]
    for n, a in enumerate((own, sib)):
        near[n] = a[:, :part]
        far[n] = a[:, part:]
    b_far[...] = b_own[:, part:]


def stack_kernel(near, far, *refs):
    o_ref = refs[-1]
    o_ref[:2] = near[...]
    o_ref[2:] = far[...]


def grads_kernel(c0, c1, c2, c3, g0, g1, g2, g3, aside, o_ref):
    for part in range(4):
        ks = slice(part * 256, part * 256 + 256)
        total = dot(c0[:, ks], g0[...], 0, 0) + dot(c1[:, ks], g1[...], 0, 0)
        total += dot(c2[:, ks], g2[...], 0, 0) + dot(c3[:, ks], g3[...], 0, 0)
        o_ref[ks, :] = total.astype(BF)


def live_kernel(y_ref, lens, parts, *refs):
    o_ref = refs[-1]
    total = parts[0].astype(F32)
    for n in range(1, 16):
        total += parts[n].astype(F32)
    col = lax.broadcasted_iota(jnp.int32, (1, 512), 1)
    pos = (col // 32 % 4) * 256 + col // 256 * 128 + y_ref[0] * 32 + col % 32
    limit = jnp.where(col % 256 < 128, lens[0], lens[1])
    total = jnp.where(pos < limit, total, 0.0).astype(BF)
    for n in range(8):
        o_ref[n] = total


def acts_kernel(xh_ref, a_ref, own, own_far, b1, b2, b3a, b3b, keep, send):
    part = a_ref.shape[3]
    rows = [(0, own, slice(0, part)), (80, own_far, slice(0, part))]
    rows += [(160, b1, slice(0, part)), (320, b2, slice(0, part))]
    for xh in range(2):
        cols = slice(xh * 256, xh * 256 + 256)
        for core, out in enumerate((keep, send)):
            tokens = a_ref[:, (xh_ref[0] + xh) % 2 * 2 + core].reshape(256, part)
            for place, b, c in rows:
                out[place : place + b.shape[0], cols] = dot(b[:, c], tokens, 1, 1)
            out[480:560, cols] = dot(b3a[...], tokens, 1, 1)
            out[560:, cols] = dot(b3b[...], tokens, 1, 1)


def add_kernel(a, b, keep, send):
    total = a[...] + b[...]
    keep[...] = total
    send[...] = total.astype(BF)


def seq_kernel(s_ref, ra, rb, rg, o_ref):
    for s in range(2):
        near, far = slice(s * 128, s * 128 + 128), slice(s * 128 + 256, s * 128 + 384)
        right = jnp.concatenate([rg[:, near], rg[:, far]], axis=1)
        for dx in range(2):
            mine, other = slice(dx * 80, dx * 80 + 80), slice(80 - dx * 80, 160 - dx * 80)
            left = [ra[mine, cols] + rb[other, cols].astype(F32) for cols in (near, far)]
            left = jnp.concatenate(left, axis=1).astype(BF)
            o_ref[(s_ref[4] + dx) % 2, 0, s] = dot(left, right, 1, 1).astype(BF)


def sequences(xh, y, ra, rb, rg):
    spec = pltpu.PrefetchScalarGridSpec(
        num_scalar_prefetch=1,
        grid=(4,),
        in_specs=[
            pl.BlockSpec((160, 512), lambda n, s: (n, 0)),
            pl.BlockSpec((160, 512), lambda n, s: (n, 0)),
            pl.BlockSpec((512, 512), lambda n, s: (0, 0)),
        ],
        out_specs=pl.BlockSpec((2, 1, 2, 80, 512), lambda n, s: (0, s[n], 0, 0, 0)),
    )
    return pl.pallas_call(
        seq_kernel,
        grid_spec=spec,
        out_shape=arr(2, 4, 2, 80, 512),
        compiler_params=WIDE,
        name="seq",
    )(jnp.stack([(y + dy + 4) % 4 for dy in ROWS] + [xh]), ra, rb, rg).reshape(8, 2, 80, 512)


def sum_kernel(parts, o_ref):
    for xh in range(2):
        total = parts[xh * 4].astype(F32)
        for y in range(1, 4):
            total += parts[xh * 4 + y].astype(F32)
        o_ref[:, :, xh * 512 : xh * 512 + 512] = total.astype(BF)


def call(kernel, out, name, args, scalars=(), aside=()):
    specs = [SMEM] * len(scalars) + [VMEM] * len(args) + [pl.BlockSpec(memory_space=pl.ANY)] * len(aside)
    return pl.pallas_call(
        kernel,
        out_shape=out,
        in_specs=specs,
        out_specs=jax.tree.map(lambda _: VMEM, out),
        compiler_params=ROOM,
        name=name,
    )(*scalars, *args, *aside)


def arr(*shape):
    return jax.ShapeDtypeStruct(shape, BF)


def per_device(activations, out_grads, basis_in, basis_out, block_ids, seq_lens, query_grads):
    xl, core, xh, y = (lax.axis_index(a).astype(jnp.int32) for a in ("xl", "core", "xh", "y"))
    slots, features = activations.shape
    part = features // 4
    place = [xh[None], core[None]]
    cuts = [arr(slots, 2 * part), arr(slots, 2 * part), arr(80, 2 * part)]
    chosen, g0, g1, g2, g3 = pick(block_ids, y, basis_out, out_grads)
    a_own, a_sib, b_own = call(cut_kernel, cuts, "cut", [activations, basis_in], place, [g0])
    a_sib = shift(a_sib, core=1)
    c1, c2 = shift(chosen, y=1), shift(chosen, y=-1)
    near, far, b_far = call(pair_kernel, [arr(2, slots, part)] * 2 + [arr(80, part)], "pair", [a_own, a_sib, b_own], (), [g0])
    far, b_far = shift(far, xh=1), shift(b_far, xh=1)
    acts = call(stack_kernel, arr(4, slots, part), "stack", [near, far], (), [c1, c2])
    acts = lax.all_gather(acts, "z", axis=0, tiled=False)
    g1, g2, g3 = shift(g1, y=1), shift(g2, y=-1), shift(g3, y=2)
    c3 = shift(c2, y=-1)

    b0 = jnp.concatenate([b_own[:, :part], b_far])
    partial = call(grads_kernel, arr(1024, 512), "grads", [chosen, c1, c2, c3, g0, g1, g2, g3], (), [b0])
    b1, b2 = shift(b0, y=1), shift(b0, y=-1)
    b3a, b3b = shift(b1[:80], y=1), shift(b2[80:], y=-1)
    parts = lax.all_to_all(partial.reshape(16, 64, 512), ("xh", "z"), split_axis=0, concat_axis=0, tiled=True)
    wide = jax.ShapeDtypeStruct((640, 512), F32)
    keep, send = call(acts_kernel, [wide, wide], "acts", [acts, b_own, b_far, b1, b2, b3a, b3b], [xh[None]])
    keep, send = call(add_kernel, [wide, arr(640, 512)], "add", [keep, shift(send, core=1)])
    rb = shift(send, xh=1)
    copies = call(live_kernel, arr(8, 64, 512), "live", [parts], [y[None], seq_lens], [send])
    rotated = lax.all_to_all(copies, "z", split_axis=0, concat_axis=0, tiled=True).reshape(512, 512)

    tiles = sequences(xh, y, keep, rb, rotated)
    got = lax.all_to_all(tiles, ("xh", "y"), split_axis=0, concat_axis=0, tiled=True)
    seq_grads = call(sum_kernel, arr(2, 80, 1024), "sums", [got])

    sibling = shift(seq_grads, core=1)
    across = shift(seq_grads, xl=1)
    diagonal = shift(across, core=1)

    def score(grads):
        return jnp.einsum("sik,qik->sq", grads, query_grads, preferred_element_type=F32)

    scored = jnp.stack([score(seq_grads), score(sibling), score(across), score(diagonal)])
    here = xl * 2 + core
    scores = jnp.concatenate(
        [lax.dynamic_index_in_dim(scored, here ^ d, 0, keepdims=False) for d in range(4)], axis=0
    )
    return jnp.sum(spread(scores, ("z", "xh", "y"), 64), axis=0)


def solution(mesh):
    fine = Mesh(mesh.devices.reshape(2, 2, 8, 2, 4), ("xl", "core", "z", "xh", "y"))
    dp, eig = ("xl", "core"), ("z", "xh", "y")
    in_specs = (
        P(dp + eig, None),
        P(eig, dp),
        P(eig, None),
        P(eig, None),
        P(),
        P(dp),
        P(dp, eig, None),
    )
    return jax.shard_map(
        per_device, mesh=fine, in_specs=in_specs, out_specs=P(None, dp), check_vma=False
    )
```

```python
import jax
import jax.numpy as jnp
from jax import lax
from jax.experimental import pallas as pl
from jax.experimental.pallas import tpu as pltpu
from jax.sharding import Mesh, PartitionSpec as P

BLOCK = 128
LEN = 1024
BF = jnp.bfloat16
F32 = jnp.float32
SIZES = {"xl": 2, "core": 2, "z": 8, "xh": 2, "y": 4}
ROWS = (0, -1, 1, 2)
VMEM = pl.BlockSpec(memory_space=pltpu.VMEM)
SMEM = pl.BlockSpec(memory_space=pltpu.SMEM)
TINY = pl.CostEstimate(flops=1, bytes_accessed=1, transcendentals=0)
WIDE = pltpu.CompilerParams(vmem_limit_bytes=60 * 1024 * 1024)
ROOM = pltpu.CompilerParams(vmem_limit_bytes=10 * 1024 * 1024)


def shift(x, **by):
    axes = tuple(by)
    count = 1
    for a in axes:
        count *= SIZES[a]
    pairs = []
    for source in range(count):
        rest, target, scale = source, 0, 1
        for a in reversed(axes):
            target += (rest % SIZES[a] + by[a]) % SIZES[a] * scale
            rest //= SIZES[a]
            scale *= SIZES[a]
        pairs.append((source, target))
    return lax.ppermute(x, axes, pairs)


def spread(x, axes, count):
    return lax.all_to_all(
        jnp.broadcast_to(x[None], (count,) + x.shape), axes, split_axis=0, concat_axis=0, tiled=True
    )


def dot(a, b, ca, cb):
    return lax.dot_general(a, b, (((ca,), (cb,)), ((), ())), preferred_element_type=F32)


def reorder(y, g_ref, outs):
    lane = lax.broadcasted_iota(jnp.int32, (1, 128), 1) // 32
    for xh in range(2):
        for part in range(2):
            start = part * 1024 + xh * 128
            cols = [g_ref[:, start + j * 256 : start + j * 256 + 128].astype(F32) for j in range(4)]
            place = xh * 256 + part * 128
            for o_ref, off, dy in outs:
                total = None
                for j in range(4):
                    moved = pltpu.roll(cols[j], ((j - dy - y + 8) % 4) * 32, 1)
                    total = moved if total is None else jnp.where(lane == j, moved, total)
                o_ref[:, off + place : off + place + 128] = total.astype(BF)


def pick_kernel(s_ref, *refs):
    picked, g_ref, chosen, g0, g1, g2, g3 = refs[:8], *refs[8:]
    for n, p in enumerate(picked):
        chosen[:, n * 128 : n * 128 + 128] = p[...]
    reorder(s_ref[8], g_ref, ((g1, 0, 1), (g2, 0, -1), (g3, 0, 2), (g0, 0, 0)))


def pick(block_ids, y, basis_out, out_grads):
    rows, tokens = out_grads.shape
    whole = lambda width: pl.BlockSpec((rows, width), lambda g, s: (0, 0))
    widths = (1024, 512, 512, 512, 512)
    spec = pltpu.PrefetchScalarGridSpec(
        num_scalar_prefetch=1,
        grid=(1,),
        in_specs=[pl.BlockSpec((rows, BLOCK), lambda g, s, n=n: (0, s[n])) for n in range(8)] + [whole(tokens)],
        out_specs=[whole(w) for w in widths],
    )
    return pl.pallas_call(
        pick_kernel,
        grid_spec=spec,
        out_shape=[arr(rows, w) for w in widths],
        compiler_params=WIDE,
        name="pick",
    )(jnp.concatenate([block_ids, y[None]]), *[basis_out] * 8, out_grads)


def halve_kernel(s_ref, b_ref, o_ref):
    o_ref[...] = b_ref[...]


def halve(core, basis_in):
    rows, half = basis_in.shape[0], basis_in.shape[1] // 2
    spec = pltpu.PrefetchScalarGridSpec(
        num_scalar_prefetch=1,
        grid=(1,),
        in_specs=[pl.BlockSpec((rows, half), lambda g, s: (0, s[0]))],
        out_specs=pl.BlockSpec((rows, half), lambda g, s: (0, 0)),
    )
    return pl.pallas_call(
        halve_kernel, grid_spec=spec, out_shape=arr(rows, half), compiler_params=ROOM, name="halve"
    )(core[None], basis_in)


def cut_kernel(core_ref, a_ref, *refs):
    o_ref = refs[-1]
    half = o_ref.shape[1]
    o_ref[...] = a_ref[:, pl.ds(pl.multiple_of((1 - core_ref[0]) * half, 128), half)]


def join_kernel(b1, b2, *refs):
    o_ref = refs[-1]
    o_ref[:80, :] = b1[...]
    o_ref[80:, :] = b2[...]


def grads_kernel(c0, c1, c2, c3, g0, g1, g2, g3, *refs):
    o_ref = refs[-1]
    for part in range(4):
        ks = slice(part * 256, part * 256 + 256)
        total = dot(c0[:, ks], g0[...], 0, 0) + dot(c1[:, ks], g1[...], 0, 0)
        total += dot(c2[:, ks], g2[...], 0, 0) + dot(c3[:, ks], g3[...], 0, 0)
        o_ref[ks, :] = total.astype(BF)


def live_kernel(y_ref, lens, parts, *refs):
    o_ref = refs[-1]
    total = parts[0].astype(F32)
    for n in range(1, 16):
        total += parts[n].astype(F32)
    col = lax.broadcasted_iota(jnp.int32, (1, 512), 1)
    pos = (col // 32 % 4) * 256 + col // 256 * 128 + y_ref[0] * 32 + col % 32
    limit = jnp.where(col % 256 < 128, lens[0], lens[1])
    total = jnp.where(pos < limit, total, 0.0).astype(BF)
    for n in range(8):
        o_ref[n] = total


def acts_kernel(core_ref, a_ref, sib, b0, far0, near, far, b3, far3, keep, send):
    half = sib.shape[1]
    mine = a_ref[:, pl.ds(pl.multiple_of(core_ref[0] * half, 128), half)]
    for tokens, out in ((sib[...], send), (mine, keep)):
        for n, (b, r) in enumerate(((b0, 0), (far0, 0), (near, 0), (far, 0), (near, 80), (far, 80), (b3, 0), (far3, 0))):
            out[n * 80 : n * 80 + 80, :] = dot(b[r : r + 80, :], tokens, 1, 1)


def add_kernel(a, b, o_ref):
    o_ref[...] = (a[...] + b[...]).astype(BF)


def seq_kernel(xh_ref, y_ref, ra, rb, rg, o_ref):
    xh = xh_ref[0]
    for s in range(2):
        near = rg[:, pl.ds(pl.multiple_of(xh * 256 + s * 128, 128), 128)]
        far = rg[:, pl.ds(pl.multiple_of((1 - xh) * 256 + s * 128, 128), 128)]
        cols = slice(s * 128, s * 128 + 128)
        right = jnp.concatenate([near, far], axis=1)
        for n, dy in enumerate(ROWS):
            for dx in range(2):
                mine = ra[n * 160 + dx * 80 : n * 160 + dx * 80 + 80, cols]
                other = rb[n * 160 + 80 - dx * 80 : n * 160 + 160 - dx * 80, cols]
                left = jnp.concatenate([mine, other], axis=1)
                target = (xh + dx) % 2 * 4 + (y_ref[0] + dy + 4) % 4
                o_ref[target, s] = dot(left, right, 1, 1).astype(BF)


def sum_kernel(parts, o_ref):
    for xh in range(2):
        total = parts[xh * 4].astype(F32)
        for y in range(1, 4):
            total += parts[xh * 4 + y].astype(F32)
        o_ref[:, :, xh * 512 : xh * 512 + 512] = total.astype(BF)


def call(kernel, out, name, args, scalars=(), aside=()):
    specs = [SMEM] * len(scalars) + [VMEM] * len(args) + [pl.BlockSpec(memory_space=pl.ANY)] * len(aside)
    return pl.pallas_call(
        kernel,
        out_shape=out,
        in_specs=specs,
        out_specs=jax.tree.map(lambda _: VMEM, out),
        compiler_params=ROOM,
        name=name,
        cost_estimate=TINY,
    )(*scalars, *args, *aside)


def arr(*shape):
    return jax.ShapeDtypeStruct(shape, BF)


def per_device(activations, out_grads, basis_in, basis_out, block_ids, seq_lens, query_grads):
    xl, core, xh, y = (lax.axis_index(a).astype(jnp.int32) for a in ("xl", "core", "xh", "y"))
    acts = lax.all_gather(activations, "z", axis=0, tiled=True)
    half = basis_in.shape[1] // 2
    b0 = halve(core, basis_in)
    b1, b2 = shift(b0, y=1), shift(b0, y=-1)
    far0 = shift(b0, xl=1, xh=1)

    chosen, g0, g1, g2, g3 = pick(block_ids, y, basis_out, out_grads)
    c1, c2 = shift(chosen, y=1), shift(chosen, y=-1)
    near = call(join_kernel, arr(160, half), "join", [b1, b2], (), [c1, c2])
    far = shift(near, xl=1, xh=1)
    g1, g2, g3 = shift(g1, y=1), shift(g2, y=-1), shift(g3, y=2)
    c3 = shift(c2, y=-1)
    partial = call(grads_kernel, arr(1024, 512), "grads", [chosen, c1, c2, c3, g0, g1, g2, g3], (), [far, far0])
    b3 = shift(b1, y=1)
    far3 = shift(far[:80], y=1)
    parts = lax.all_to_all(partial.reshape(16, 64, 512), ("xh", "z"), split_axis=0, concat_axis=0, tiled=True)
    wide = jax.ShapeDtypeStruct((640, 256), F32)
    sib = shift(call(cut_kernel, arr(256, half), "cut", [acts], [core[None]], [partial]), core=1)
    keep, send = call(acts_kernel, [wide, wide], "acts", [acts, sib, b0, far0, near, far, b3, far3], [core[None]])
    ra = call(add_kernel, arr(640, 256), "add", [keep, shift(send, core=1)])
    rb = shift(ra, xh=1)
    copies = call(live_kernel, arr(8, 64, 512), "live", [parts], [y[None], seq_lens], [ra])
    rotated = lax.all_to_all(copies, "z", split_axis=0, concat_axis=0, tiled=True).reshape(512, 512)

    tiles = call(seq_kernel, arr(8, 2, 80, 512), "seq", [ra, rb, rotated], [xh[None], y[None]])
    got = lax.all_to_all(tiles, ("xh", "y"), split_axis=0, concat_axis=0, tiled=True)
    seq_grads = call(sum_kernel, arr(2, 80, 1024), "sums", [got])

    sibling = shift(seq_grads, core=1)
    across = shift(seq_grads, xl=1)
    diagonal = shift(across, core=1)

    def score(grads):
        return jnp.einsum("sik,qik->sq", grads, query_grads, preferred_element_type=F32)

    scored = jnp.stack([score(seq_grads), score(sibling), score(across), score(diagonal)])
    here = xl * 2 + core
    scores = jnp.concatenate(
        [lax.dynamic_index_in_dim(scored, here ^ d, 0, keepdims=False) for d in range(4)], axis=0
    )
    return jnp.sum(spread(scores, ("z", "xh", "y"), 64), axis=0)


def solution(mesh):
    fine = Mesh(mesh.devices.reshape(2, 2, 8, 2, 4), ("xl", "core", "z", "xh", "y"))
    dp, eig = ("xl", "core"), ("z", "xh", "y")
    in_specs = (
        P(dp + eig, None),
        P(eig, dp),
        P(eig, None),
        P(eig, None),
        P(),
        P(dp),
        P(dp, eig, None),
    )
    return jax.shard_map(
        per_device, mesh=fine, in_specs=in_specs, out_specs=P(None, dp), check_vma=False
    )
```

```python
import jax
import jax.numpy as jnp
from jax import lax
from jax.experimental import pallas as pl
from jax.experimental.pallas import tpu as pltpu
from jax.sharding import Mesh, PartitionSpec as P

BLOCK = 128
LEN = 1024
BF = jnp.bfloat16
F32 = jnp.float32
SIZES = {"xl": 2, "core": 2, "z": 8, "xh": 2, "y": 4}
ROWS = (0, -1, 1, 2)
VMEM = pl.BlockSpec(memory_space=pltpu.VMEM)
SMEM = pl.BlockSpec(memory_space=pltpu.SMEM)
TINY = pl.CostEstimate(flops=1, bytes_accessed=1, transcendentals=0)
WIDE = pltpu.CompilerParams(vmem_limit_bytes=60 * 1024 * 1024)
ROOM = pltpu.CompilerParams(vmem_limit_bytes=10 * 1024 * 1024)


def shift(x, **by):
    axes = tuple(by)
    count = 1
    for a in axes:
        count *= SIZES[a]
    pairs = []
    for source in range(count):
        rest, target, scale = source, 0, 1
        for a in reversed(axes):
            target += (rest % SIZES[a] + by[a]) % SIZES[a] * scale
            rest //= SIZES[a]
            scale *= SIZES[a]
        pairs.append((source, target))
    return lax.ppermute(x, axes, pairs)


def spread(x, axes, count):
    return lax.all_to_all(
        jnp.broadcast_to(x[None], (count,) + x.shape), axes, split_axis=0, concat_axis=0, tiled=True
    )


def dot(a, b, ca, cb):
    return lax.dot_general(a, b, (((ca,), (cb,)), ((), ())), preferred_element_type=F32)


def reorder(y, g_ref, outs):
    lane = lax.broadcasted_iota(jnp.int32, (1, 128), 1) // 32
    for xh in range(2):
        for part in range(2):
            start = part * 1024 + xh * 128
            cols = [g_ref[:, start + j * 256 : start + j * 256 + 128].astype(F32) for j in range(4)]
            place = xh * 256 + part * 128
            for o_ref, off, dy in outs:
                total = None
                for j in range(4):
                    moved = pltpu.roll(cols[j], ((j - dy - y + 8) % 4) * 32, 1)
                    total = moved if total is None else jnp.where(lane == j, moved, total)
                o_ref[:, off + place : off + place + 128] = total.astype(BF)


def pick_kernel(s_ref, *refs):
    picked, g_ref, chosen, g0, g1, g2, g3 = refs[:8], *refs[8:]
    for n, p in enumerate(picked):
        chosen[:, n * 128 : n * 128 + 128] = p[...]
    reorder(s_ref[8], g_ref, ((g1, 0, 1), (g2, 0, -1), (g3, 0, 2), (g0, 0, 0)))


def pick(block_ids, y, basis_out, out_grads):
    rows, tokens = out_grads.shape
    whole = lambda width: pl.BlockSpec((rows, width), lambda g, s: (0, 0))
    widths = (1024, 512, 512, 512, 512)
    spec = pltpu.PrefetchScalarGridSpec(
        num_scalar_prefetch=1,
        grid=(1,),
        in_specs=[pl.BlockSpec((rows, BLOCK), lambda g, s, n=n: (0, s[n])) for n in range(8)] + [whole(tokens)],
        out_specs=[whole(w) for w in widths],
    )
    return pl.pallas_call(
        pick_kernel,
        grid_spec=spec,
        out_shape=[arr(rows, w) for w in widths],
        compiler_params=WIDE,
        name="pick",
    )(jnp.concatenate([block_ids, y[None]]), *[basis_out] * 8, out_grads)


def halve_kernel(s_ref, b_ref, o_ref):
    o_ref[...] = b_ref[...]


def halve(core, basis_in):
    rows, half = basis_in.shape[0], basis_in.shape[1] // 2
    spec = pltpu.PrefetchScalarGridSpec(
        num_scalar_prefetch=1,
        grid=(1,),
        in_specs=[pl.BlockSpec((rows, half), lambda g, s: (0, s[0]))],
        out_specs=pl.BlockSpec((rows, half), lambda g, s: (0, 0)),
    )
    return pl.pallas_call(
        halve_kernel, grid_spec=spec, out_shape=arr(rows, half), compiler_params=ROOM, name="halve"
    )(core[None], basis_in)


def cut_kernel(core_ref, a_ref, *refs):
    o_ref = refs[-1]
    half = o_ref.shape[1]
    o_ref[...] = a_ref[:, pl.ds(pl.multiple_of((1 - core_ref[0]) * half, 128), half)]


def grads_kernel(c0, c1, c2, c3, g0, g1, g2, g3, b_own, b_far, o_ref, b0):
    b0[:80, :] = b_own[...]
    b0[80:, :] = b_far[...]
    for part in range(4):
        ks = slice(part * 256, part * 256 + 256)
        total = dot(c0[:, ks], g0[...], 0, 0) + dot(c1[:, ks], g1[...], 0, 0)
        total += dot(c2[:, ks], g2[...], 0, 0) + dot(c3[:, ks], g3[...], 0, 0)
        o_ref[ks, :] = total.astype(BF)


def live_kernel(y_ref, lens, parts, *refs):
    o_ref = refs[-1]
    total = parts[0].astype(F32)
    for n in range(1, 16):
        total += parts[n].astype(F32)
    col = lax.broadcasted_iota(jnp.int32, (1, 512), 1)
    pos = (col // 32 % 4) * 256 + col // 256 * 128 + y_ref[0] * 32 + col % 32
    limit = jnp.where(col % 256 < 128, lens[0], lens[1])
    total = jnp.where(pos < limit, total, 0.0).astype(BF)
    for n in range(8):
        o_ref[n] = total


def acts_kernel(core_ref, a_ref, sib, b0, b1, b2, b3a, b3b, keep, send):
    half = sib.shape[1]
    mine = a_ref[:, pl.ds(pl.multiple_of(core_ref[0] * half, 128), half)]
    for tokens, out in ((sib[...], send), (mine, keep)):
        for n, b in enumerate((b0, b1, b2)):
            out[n * 160 : n * 160 + 160, :] = dot(b[...], tokens, 1, 1)
        out[480:, :] = dot(b3a[...], tokens[:, : half // 2], 1, 1) + dot(b3b[...], tokens[:, half // 2 :], 1, 1)


def add_kernel(a, b, o_ref):
    o_ref[...] = (a[...] + b[...]).astype(BF)


def seq_kernel(xh_ref, y_ref, ra, rb, rg, o_ref):
    xh = xh_ref[0]
    for s in range(2):
        near = rg[:, pl.ds(pl.multiple_of(xh * 256 + s * 128, 128), 128)]
        far = rg[:, pl.ds(pl.multiple_of((1 - xh) * 256 + s * 128, 128), 128)]
        cols = slice(s * 128, s * 128 + 128)
        right = jnp.concatenate([near, far], axis=1)
        for n, dy in enumerate(ROWS):
            for dx in range(2):
                mine = ra[n * 160 + dx * 80 : n * 160 + dx * 80 + 80, cols]
                other = rb[n * 160 + 80 - dx * 80 : n * 160 + 160 - dx * 80, cols]
                left = jnp.concatenate([mine, other], axis=1)
                target = (xh + dx) % 2 * 4 + (y_ref[0] + dy + 4) % 4
                o_ref[target, s] = dot(left, right, 1, 1).astype(BF)


def sum_kernel(parts, o_ref):
    for xh in range(2):
        total = parts[xh * 4].astype(F32)
        for y in range(1, 4):
            total += parts[xh * 4 + y].astype(F32)
        o_ref[:, :, xh * 512 : xh * 512 + 512] = total.astype(BF)


def call(kernel, out, name, args, scalars=(), aside=()):
    specs = [SMEM] * len(scalars) + [VMEM] * len(args) + [pl.BlockSpec(memory_space=pl.ANY)] * len(aside)
    return pl.pallas_call(
        kernel,
        out_shape=out,
        in_specs=specs,
        out_specs=jax.tree.map(lambda _: VMEM, out),
        compiler_params=ROOM,
        name=name,
        cost_estimate=TINY,
    )(*scalars, *args, *aside)


def arr(*shape):
    return jax.ShapeDtypeStruct(shape, BF)


def per_device(activations, out_grads, basis_in, basis_out, block_ids, seq_lens, query_grads):
    xl, core, xh, y = (lax.axis_index(a).astype(jnp.int32) for a in ("xl", "core", "xh", "y"))
    acts = lax.all_gather(activations, "z", axis=0, tiled=True)
    half = basis_in.shape[1] // 2
    chosen, g0, g1, g2, g3 = pick(block_ids, y, basis_out, out_grads)
    c1, c2 = shift(chosen, y=1), shift(chosen, y=-1)
    g1, g2, g3 = shift(g1, y=1), shift(g2, y=-1), shift(g3, y=2)
    c3 = shift(c2, y=-1)
    b_own = halve(core, basis_in)
    b_far = shift(b_own, xl=1, xh=1)
    partial, b0 = call(
        grads_kernel, [arr(1024, 512), arr(160, half)], "grads", [chosen, c1, c2, c3, g0, g1, g2, g3, b_own, b_far]
    )
    b1, b2 = shift(b0, y=1), shift(b0, y=-1)
    b3a, b3b = shift(b1[:, : half // 2], y=1), shift(b2[:, half // 2 :], y=-1)
    parts = lax.all_to_all(partial.reshape(16, 64, 512), ("xh", "z"), split_axis=0, concat_axis=0, tiled=True)
    wide = jax.ShapeDtypeStruct((640, 256), F32)
    sib = shift(call(cut_kernel, arr(256, half), "cut", [acts], [core[None]], [b1, b2]), core=1)
    keep, send = call(acts_kernel, [wide, wide], "acts", [acts, sib, b0, b1, b2, b3a, b3b], [core[None]])
    ra = call(add_kernel, arr(640, 256), "add", [keep, shift(send, core=1)])
    rb = shift(ra, xh=1)
    copies = call(live_kernel, arr(8, 64, 512), "live", [parts], [y[None], seq_lens], [send])
    rotated = lax.all_to_all(copies, "z", split_axis=0, concat_axis=0, tiled=True).reshape(512, 512)

    tiles = call(seq_kernel, arr(8, 2, 80, 512), "seq", [ra, rb, rotated], [xh[None], y[None]])
    got = lax.all_to_all(tiles, ("xh", "y"), split_axis=0, concat_axis=0, tiled=True)
    seq_grads = call(sum_kernel, arr(2, 80, 1024), "sums", [got])

    sibling = shift(seq_grads, core=1)
    across = shift(seq_grads, xl=1)
    diagonal = shift(across, core=1)

    def score(grads):
        return jnp.einsum("sik,qik->sq", grads, query_grads, preferred_element_type=F32)

    scored = jnp.stack([score(seq_grads), score(sibling), score(across), score(diagonal)])
    here = xl * 2 + core
    scores = jnp.concatenate(
        [lax.dynamic_index_in_dim(scored, here ^ d, 0, keepdims=False) for d in range(4)], axis=0
    )
    return jnp.sum(spread(scores, ("z", "xh", "y"), 64), axis=0)


def solution(mesh):
    fine = Mesh(mesh.devices.reshape(2, 2, 8, 2, 4), ("xl", "core", "z", "xh", "y"))
    dp, eig = ("xl", "core"), ("z", "xh", "y")
    in_specs = (
        P(dp + eig, None),
        P(eig, dp),
        P(eig, None),
        P(eig, None),
        P(),
        P(dp),
        P(dp, eig, None),
    )
    return jax.shard_map(
        per_device, mesh=fine, in_specs=in_specs, out_specs=P(None, dp), check_vma=False
    )
```

```python
import jax
import jax.numpy as jnp
from jax import lax
from jax.experimental import pallas as pl
from jax.experimental.pallas import tpu as pltpu
from jax.sharding import Mesh, PartitionSpec as P

BLOCK = 128
LEN = 1024
BF = jnp.bfloat16
F32 = jnp.float32
SIZES = {"xl": 2, "core": 2, "z": 8, "xh": 2, "y": 4}
ROWS = (0, -1, 1, 2)
VMEM = pl.BlockSpec(memory_space=pltpu.VMEM)
SMEM = pl.BlockSpec(memory_space=pltpu.SMEM)
TINY = pl.CostEstimate(flops=1, bytes_accessed=1, transcendentals=0)
WIDE = pltpu.CompilerParams(vmem_limit_bytes=60 * 1024 * 1024)
ROOM = pltpu.CompilerParams(vmem_limit_bytes=10 * 1024 * 1024)


def shift(x, **by):
    axes = tuple(by)
    count = 1
    for a in axes:
        count *= SIZES[a]
    pairs = []
    for source in range(count):
        rest, target, scale = source, 0, 1
        for a in reversed(axes):
            target += (rest % SIZES[a] + by[a]) % SIZES[a] * scale
            rest //= SIZES[a]
            scale *= SIZES[a]
        pairs.append((source, target))
    return lax.ppermute(x, axes, pairs)


def spread(x, axes, count):
    return lax.all_to_all(
        jnp.broadcast_to(x[None], (count,) + x.shape), axes, split_axis=0, concat_axis=0, tiled=True
    )


def dot(a, b, ca, cb):
    return lax.dot_general(a, b, (((ca,), (cb,)), ((), ())), preferred_element_type=F32)


def reorder(y, g_ref, outs):
    lane = lax.broadcasted_iota(jnp.int32, (1, 128), 1) // 32
    for xh in range(2):
        for part in range(2):
            start = part * 1024 + xh * 128
            cols = [g_ref[:, start + j * 256 : start + j * 256 + 128].astype(F32) for j in range(4)]
            place = xh * 256 + part * 128
            for o_ref, off, dy in outs:
                total = None
                for j in range(4):
                    moved = pltpu.roll(cols[j], ((j - dy - y + 8) % 4) * 32, 1)
                    total = moved if total is None else jnp.where(lane == j, moved, total)
                o_ref[:, off + place : off + place + 128] = total.astype(BF)


def pick_kernel(ids, y_ref, core_ref, *refs):
    picked, g_ref, chosen, half, g0, g1, g2, g3 = refs[:8], *refs[8:]
    for n, p in enumerate(picked):
        chosen[:, n * 128 : n * 128 + 128] = p[...]
    half[...] = chosen[:, pl.ds(pl.multiple_of(core_ref[0] * 512, 128), 512)]
    reorder(y_ref[0], g_ref, ((g1, 0, 1), (g2, 0, -1), (g3, 0, 2), (g0, 0, 0)))


def pick(block_ids, y, core, basis_out, out_grads):
    rows, tokens = out_grads.shape
    whole = lambda width: pl.BlockSpec((rows, width), lambda g, *s: (0, 0))
    widths = (1024, 512, 512, 512, 512, 512)
    spec = pltpu.PrefetchScalarGridSpec(
        num_scalar_prefetch=3,
        grid=(1,),
        in_specs=[pl.BlockSpec((rows, BLOCK), lambda g, s, y, c, n=n: (0, s[n])) for n in range(8)] + [whole(tokens)],
        out_specs=[whole(w) for w in widths],
    )
    return pl.pallas_call(
        pick_kernel,
        grid_spec=spec,
        out_shape=[arr(rows, w) for w in widths],
        compiler_params=WIDE,
        name="pick",
    )(block_ids, y[None], core[None], *[basis_out] * 8, out_grads)


def halve_kernel(s_ref, b_ref, o_ref):
    o_ref[...] = b_ref[...]


def halve(core, basis_in):
    rows, half = basis_in.shape[0], basis_in.shape[1] // 2
    spec = pltpu.PrefetchScalarGridSpec(
        num_scalar_prefetch=1,
        grid=(1,),
        in_specs=[pl.BlockSpec((rows, half), lambda g, s: (0, s[0]))],
        out_specs=pl.BlockSpec((rows, half), lambda g, s: (0, 0)),
    )
    return pl.pallas_call(
        halve_kernel, grid_spec=spec, out_shape=arr(rows, half), compiler_params=ROOM, name="halve"
    )(core[None], basis_in)


def cut_kernel(core_ref, a_ref, *refs):
    o_ref = refs[-1]
    half = o_ref.shape[1]
    o_ref[...] = a_ref[:, pl.ds(pl.multiple_of((1 - core_ref[0]) * half, 128), half)]


def grads_kernel(core_ref, c0, h1, h2, h3, o1, o2, o3, g0, g1, g2, g3, b_own, b_far, o_ref, b0):
    b0[:80, :] = b_own[...]
    b0[80:, :] = b_far[...]
    for which, (a1, a2, a3) in ((core_ref[0], (h1, h2, h3)), (1 - core_ref[0], (o1, o2, o3))):
        for off in (0, 256):
            ks = slice(off, off + 256)
            place = pl.ds(pl.multiple_of(which * 512 + off, 256), 256)
            total = dot(c0[:, place], g0[...], 0, 0) + dot(a1[:, ks], g1[...], 0, 0)
            total += dot(a2[:, ks], g2[...], 0, 0) + dot(a3[:, ks], g3[...], 0, 0)
            o_ref[place, :] = total.astype(BF)


def live_kernel(y_ref, lens, parts, *refs):
    o_ref = refs[-1]
    total = parts[0].astype(F32)
    for n in range(1, 16):
        total += parts[n].astype(F32)
    col = lax.broadcasted_iota(jnp.int32, (1, 512), 1)
    pos = (col // 32 % 4) * 256 + col // 256 * 128 + y_ref[0] * 32 + col % 32
    limit = jnp.where(col % 256 < 128, lens[0], lens[1])
    total = jnp.where(pos < limit, total, 0.0).astype(BF)
    for n in range(8):
        o_ref[n] = total


def acts_kernel(core_ref, a_ref, sib, b0, b1, b2, b3a, b3b, keep, send):
    half = sib.shape[1]
    mine = a_ref[:, pl.ds(pl.multiple_of(core_ref[0] * half, 128), half)]
    for tokens, out in ((sib[...], send), (mine, keep)):
        for n, b in enumerate((b0, b1, b2)):
            out[n * 160 : n * 160 + 160, :] = dot(b[...], tokens, 1, 1)
        out[480:, :] = dot(b3a[...], tokens[:, : half // 2], 1, 1) + dot(b3b[...], tokens[:, half // 2 :], 1, 1)


def add_kernel(a, b, o_ref):
    o_ref[...] = (a[...] + b[...]).astype(BF)


def seq_kernel(xh_ref, y_ref, ra, rb, rg, o_ref):
    xh = xh_ref[0]
    for s in range(2):
        near = rg[:, pl.ds(pl.multiple_of(xh * 256 + s * 128, 128), 128)]
        far = rg[:, pl.ds(pl.multiple_of((1 - xh) * 256 + s * 128, 128), 128)]
        cols = slice(s * 128, s * 128 + 128)
        right = jnp.concatenate([near, far], axis=1)
        for n, dy in enumerate(ROWS):
            for dx in range(2):
                mine = ra[n * 160 + dx * 80 : n * 160 + dx * 80 + 80, cols]
                other = rb[n * 160 + 80 - dx * 80 : n * 160 + 160 - dx * 80, cols]
                left = jnp.concatenate([mine, other], axis=1)
                target = (xh + dx) % 2 * 4 + (y_ref[0] + dy + 4) % 4
                o_ref[target, s] = dot(left, right, 1, 1).astype(BF)


def sum_kernel(parts, o_ref):
    for xh in range(2):
        total = parts[xh * 4].astype(F32)
        for y in range(1, 4):
            total += parts[xh * 4 + y].astype(F32)
        o_ref[:, :, xh * 512 : xh * 512 + 512] = total.astype(BF)


def call(kernel, out, name, args, scalars=(), aside=()):
    specs = [SMEM] * len(scalars) + [VMEM] * len(args) + [pl.BlockSpec(memory_space=pl.ANY)] * len(aside)
    return pl.pallas_call(
        kernel,
        out_shape=out,
        in_specs=specs,
        out_specs=jax.tree.map(lambda _: VMEM, out),
        compiler_params=ROOM,
        name=name,
        cost_estimate=TINY,
    )(*scalars, *args, *aside)


def arr(*shape):
    return jax.ShapeDtypeStruct(shape, BF)


def per_device(activations, out_grads, basis_in, basis_out, block_ids, seq_lens, query_grads):
    xl, core, xh, y = (lax.axis_index(a).astype(jnp.int32) for a in ("xl", "core", "xh", "y"))
    acts = lax.all_gather(activations, "z", axis=0, tiled=True)
    half = basis_in.shape[1] // 2
    chosen, c0, g0, g1, g2, g3 = pick(block_ids, y, core, basis_out, out_grads)
    c1, c2 = shift(c0, y=1), shift(c0, y=-1)
    g1, g2, g3 = shift(g1, y=1), shift(g2, y=-1), shift(g3, y=2)
    c3 = shift(c2, y=-1)
    others = [shift(c, core=1) for c in (c1, c2, c3)]
    b_own = halve(core, basis_in)
    b_far = shift(b_own, xl=1, xh=1)
    partial, b0 = call(
        grads_kernel,
        [arr(1024, 512), arr(160, half)],
        "grads",
        [chosen, c1, c2, c3, *others, g0, g1, g2, g3, b_own, b_far],
        [core[None]],
    )
    b1, b2 = shift(b0, y=1), shift(b0, y=-1)
    b3a, b3b = shift(b1[:, : half // 2], y=1), shift(b2[:, half // 2 :], y=-1)
    parts = lax.all_to_all(partial.reshape(16, 64, 512), ("xh", "z"), split_axis=0, concat_axis=0, tiled=True)
    wide = jax.ShapeDtypeStruct((640, 256), F32)
    sib = shift(call(cut_kernel, arr(256, half), "cut", [acts], [core[None]], [b1, b2]), core=1)
    keep, send = call(acts_kernel, [wide, wide], "acts", [acts, sib, b0, b1, b2, b3a, b3b], [core[None]])
    ra = call(add_kernel, arr(640, 256), "add", [keep, shift(send, core=1)])
    rb = shift(ra, xh=1)
    copies = call(live_kernel, arr(8, 64, 512), "live", [parts], [y[None], seq_lens], [send])
    rotated = lax.all_to_all(copies, "z", split_axis=0, concat_axis=0, tiled=True).reshape(512, 512)

    tiles = call(seq_kernel, arr(8, 2, 80, 512), "seq", [ra, rb, rotated], [xh[None], y[None]])
    got = lax.all_to_all(tiles, ("xh", "y"), split_axis=0, concat_axis=0, tiled=True)
    seq_grads = call(sum_kernel, arr(2, 80, 1024), "sums", [got])

    sibling = shift(seq_grads, core=1)
    across = shift(seq_grads, xl=1)
    diagonal = shift(across, core=1)

    def score(grads):
        return jnp.einsum("sik,qik->sq", grads, query_grads, preferred_element_type=F32)

    scored = jnp.stack([score(seq_grads), score(sibling), score(across), score(diagonal)])
    here = xl * 2 + core
    scores = jnp.concatenate(
        [lax.dynamic_index_in_dim(scored, here ^ d, 0, keepdims=False) for d in range(4)], axis=0
    )
    return jnp.sum(spread(scores, ("z", "xh", "y"), 64), axis=0)


def solution(mesh):
    fine = Mesh(mesh.devices.reshape(2, 2, 8, 2, 4), ("xl", "core", "z", "xh", "y"))
    dp, eig = ("xl", "core"), ("z", "xh", "y")
    in_specs = (
        P(dp + eig, None),
        P(eig, dp),
        P(eig, None),
        P(eig, None),
        P(),
        P(dp),
        P(dp, eig, None),
    )
    return jax.shard_map(
        per_device, mesh=fine, in_specs=in_specs, out_specs=P(None, dp), check_vma=False
    )
```

```python
import jax
import jax.numpy as jnp
from jax import lax
from jax.experimental import pallas as pl
from jax.experimental.pallas import tpu as pltpu
from jax.sharding import Mesh, PartitionSpec as P

BLOCK = 128
LEN = 1024
BF = jnp.bfloat16
F32 = jnp.float32
SIZES = {"xl": 2, "core": 2, "z": 8, "xh": 2, "y": 4}
ROWS = (0, -1, 1, 2)
VMEM = pl.BlockSpec(memory_space=pltpu.VMEM)
SMEM = pl.BlockSpec(memory_space=pltpu.SMEM)
TINY = pl.CostEstimate(flops=1, bytes_accessed=1, transcendentals=0)
WIDE = pltpu.CompilerParams(vmem_limit_bytes=60 * 1024 * 1024)
ROOM = pltpu.CompilerParams(vmem_limit_bytes=10 * 1024 * 1024)


def shift(x, **by):
    axes = tuple(by)
    count = 1
    for a in axes:
        count *= SIZES[a]
    pairs = []
    for source in range(count):
        rest, target, scale = source, 0, 1
        for a in reversed(axes):
            target += (rest % SIZES[a] + by[a]) % SIZES[a] * scale
            rest //= SIZES[a]
            scale *= SIZES[a]
        pairs.append((source, target))
    return lax.ppermute(x, axes, pairs)


def spread(x, axes, count):
    return lax.all_to_all(
        jnp.broadcast_to(x[None], (count,) + x.shape), axes, split_axis=0, concat_axis=0, tiled=True
    )


def dot(a, b, ca, cb):
    return lax.dot_general(a, b, (((ca,), (cb,)), ((), ())), preferred_element_type=F32)


def reorder(y, g_ref, outs):
    lane = lax.broadcasted_iota(jnp.int32, (1, 128), 1) // 32
    for xh in range(2):
        for part in range(2):
            start = part * 1024 + xh * 128
            cols = [g_ref[:, start + j * 256 : start + j * 256 + 128].astype(F32) for j in range(4)]
            place = xh * 256 + part * 128
            for o_ref, off, dy in outs:
                total = None
                for j in range(4):
                    moved = pltpu.roll(cols[j], ((j - dy - y + 8) % 4) * 32, 1)
                    total = moved if total is None else jnp.where(lane == j, moved, total)
                o_ref[:, off + place : off + place + 128] = total.astype(BF)


def half_kernel(ids, core_ref, *refs):
    *picked, o_ref = refs
    for n, p in enumerate(picked):
        o_ref[:, n * 128 : n * 128 + 128] = p[...]


def pick_half(block_ids, core, basis_out):
    rows = basis_out.shape[0]
    spec = pltpu.PrefetchScalarGridSpec(
        num_scalar_prefetch=2,
        grid=(1,),
        in_specs=[pl.BlockSpec((rows, BLOCK), lambda g, s, c, n=n: (0, s[c[0] * 4 + n])) for n in range(4)],
        out_specs=pl.BlockSpec((rows, 512), lambda g, s, c: (0, 0)),
    )
    return pl.pallas_call(
        half_kernel, grid_spec=spec, out_shape=arr(rows, 512), compiler_params=WIDE, name="pick_half"
    )(block_ids, core[None], *[basis_out] * 4)


def pick_kernel(ids, y_ref, *refs):
    picked, g_ref, aside, chosen, g0, g1, g2, g3 = refs[:8], *refs[8:]
    for n, p in enumerate(picked):
        chosen[:, n * 128 : n * 128 + 128] = p[...]
    reorder(y_ref[0], g_ref, ((g1, 0, 1), (g2, 0, -1), (g3, 0, 2), (g0, 0, 0)))


def pick(block_ids, y, basis_out, out_grads, aside):
    rows, tokens = out_grads.shape
    whole = lambda width: pl.BlockSpec((rows, width), lambda g, *s: (0, 0))
    widths = (1024, 512, 512, 512, 512)
    spec = pltpu.PrefetchScalarGridSpec(
        num_scalar_prefetch=2,
        grid=(1,),
        in_specs=[pl.BlockSpec((rows, BLOCK), lambda g, s, y, n=n: (0, s[n])) for n in range(8)]
        + [whole(tokens), pl.BlockSpec(memory_space=pl.ANY)],
        out_specs=[whole(w) for w in widths],
    )
    return pl.pallas_call(
        pick_kernel,
        grid_spec=spec,
        out_shape=[arr(rows, w) for w in widths],
        compiler_params=WIDE,
        name="pick",
    )(block_ids, y[None], *[basis_out] * 8, out_grads, aside)


def halve_kernel(s_ref, b_ref, o_ref):
    o_ref[...] = b_ref[...]


def halve(core, basis_in):
    rows, half = basis_in.shape[0], basis_in.shape[1] // 2
    spec = pltpu.PrefetchScalarGridSpec(
        num_scalar_prefetch=1,
        grid=(1,),
        in_specs=[pl.BlockSpec((rows, half), lambda g, s: (0, s[0]))],
        out_specs=pl.BlockSpec((rows, half), lambda g, s: (0, 0)),
    )
    return pl.pallas_call(
        halve_kernel, grid_spec=spec, out_shape=arr(rows, half), compiler_params=ROOM, name="halve"
    )(core[None], basis_in)


def cut_kernel(core_ref, a_ref, b1, b2, o_ref, left, right):
    half = o_ref.shape[1]
    left[...] = b1[:, : half // 2]
    right[...] = b2[:, half // 2 :]
    o_ref[...] = a_ref[:, pl.ds(pl.multiple_of((1 - core_ref[0]) * half, 128), half)]


def grads_kernel(core_ref, c0, h1, h2, h3, o1, o2, o3, g0, g1, g2, g3, b_own, b_far, o_ref, b0):
    b0[:80, :] = b_own[...]
    b0[80:, :] = b_far[...]
    for which, (a1, a2, a3) in ((core_ref[0], (h1, h2, h3)), (1 - core_ref[0], (o1, o2, o3))):
        for off in (0, 256):
            ks = slice(off, off + 256)
            place = pl.ds(pl.multiple_of(which * 512 + off, 256), 256)
            total = dot(c0[:, place], g0[...], 0, 0) + dot(a1[:, ks], g1[...], 0, 0)
            total += dot(a2[:, ks], g2[...], 0, 0) + dot(a3[:, ks], g3[...], 0, 0)
            o_ref[place, :] = total.astype(BF)


def live_kernel(y_ref, lens, parts, *refs):
    o_ref = refs[-1]
    total = parts[0].astype(F32)
    for n in range(1, 16):
        total += parts[n].astype(F32)
    col = lax.broadcasted_iota(jnp.int32, (1, 512), 1)
    pos = (col // 32 % 4) * 256 + col // 256 * 128 + y_ref[0] * 32 + col % 32
    limit = jnp.where(col % 256 < 128, lens[0], lens[1])
    total = jnp.where(pos < limit, total, 0.0).astype(BF)
    for n in range(8):
        o_ref[n] = total


def acts_kernel(core_ref, a_ref, sib, b0, b1, b2, b3a, b3b, keep, send):
    half = sib.shape[1]
    mine = a_ref[:, pl.ds(pl.multiple_of(core_ref[0] * half, 128), half)]
    for tokens, out in ((sib[...], send), (mine, keep)):
        for n, b in enumerate((b0, b1, b2)):
            out[n * 160 : n * 160 + 160, :] = dot(b[...], tokens, 1, 1)
        out[480:, :] = dot(b3a[...], tokens[:, : half // 2], 1, 1) + dot(b3b[...], tokens[:, half // 2 :], 1, 1)


def add_kernel(a, b, o_ref):
    o_ref[...] = (a[...] + b[...]).astype(BF)


def seq_kernel(xh_ref, y_ref, ra, rb, rg, o_ref):
    xh = xh_ref[0]
    for s in range(2):
        near = rg[:, pl.ds(pl.multiple_of(xh * 256 + s * 128, 128), 128)]
        far = rg[:, pl.ds(pl.multiple_of((1 - xh) * 256 + s * 128, 128), 128)]
        cols = slice(s * 128, s * 128 + 128)
        right = jnp.concatenate([near, far], axis=1)
        for n, dy in enumerate(ROWS):
            for dx in range(2):
                mine = ra[n * 160 + dx * 80 : n * 160 + dx * 80 + 80, cols]
                other = rb[n * 160 + 80 - dx * 80 : n * 160 + 160 - dx * 80, cols]
                left = jnp.concatenate([mine, other], axis=1)
                target = (xh + dx) % 2 * 4 + (y_ref[0] + dy + 4) % 4
                o_ref[target, s] = dot(left, right, 1, 1).astype(BF)


def sum_kernel(parts, o_ref):
    for xh in range(2):
        total = parts[xh * 4].astype(F32)
        for y in range(1, 4):
            total += parts[xh * 4 + y].astype(F32)
        o_ref[:, :, xh * 512 : xh * 512 + 512] = total.astype(BF)


def call(kernel, out, name, args, scalars=(), aside=()):
    specs = [SMEM] * len(scalars) + [VMEM] * len(args) + [pl.BlockSpec(memory_space=pl.ANY)] * len(aside)
    return pl.pallas_call(
        kernel,
        out_shape=out,
        in_specs=specs,
        out_specs=jax.tree.map(lambda _: VMEM, out),
        compiler_params=ROOM,
        name=name,
        cost_estimate=TINY,
    )(*scalars, *args, *aside)


def arr(*shape):
    return jax.ShapeDtypeStruct(shape, BF)


def per_device(activations, out_grads, basis_in, basis_out, block_ids, seq_lens, query_grads):
    xl, core, xh, y = (lax.axis_index(a).astype(jnp.int32) for a in ("xl", "core", "xh", "y"))
    acts = lax.all_gather(activations, "z", axis=0, tiled=True)
    half = basis_in.shape[1] // 2
    c0 = pick_half(block_ids, core, basis_out)
    c1, c2 = shift(c0, y=1), shift(c0, y=-1)
    chosen, g0, g1, g2, g3 = pick(block_ids, y, basis_out, out_grads, c0)
    g1, g2, g3 = shift(g1, y=1), shift(g2, y=-1), shift(g3, y=2)
    c3 = shift(c2, y=-1)
    others = [shift(c, core=1) for c in (c1, c2, c3)]
    b_own = halve(core, basis_in)
    b_far = shift(b_own, xl=1, xh=1)
    partial, b0 = call(
        grads_kernel,
        [arr(1024, 512), arr(160, half)],
        "grads",
        [chosen, c1, c2, c3, *others, g0, g1, g2, g3, b_own, b_far],
        [core[None]],
    )
    b1, b2 = shift(b0, y=1), shift(b0, y=-1)
    parts = lax.all_to_all(partial.reshape(16, 64, 512), ("xh", "z"), split_axis=0, concat_axis=0, tiled=True)
    wide = jax.ShapeDtypeStruct((640, 256), F32)
    cuts = [arr(256, half), arr(160, half // 2), arr(160, half // 2)]
    sib, left, right = call(cut_kernel, cuts, "cut", [acts, b1, b2], [core[None]])
    sib, b3a, b3b = shift(sib, core=1), shift(left, y=1), shift(right, y=-1)
    keep, send = call(acts_kernel, [wide, wide], "acts", [acts, sib, b0, b1, b2, b3a, b3b], [core[None]])
    ra = call(add_kernel, arr(640, 256), "add", [keep, shift(send, core=1)])
    rb = shift(ra, xh=1)
    copies = call(live_kernel, arr(8, 64, 512), "live", [parts], [y[None], seq_lens], [send])
    rotated = lax.all_to_all(copies, "z", split_axis=0, concat_axis=0, tiled=True).reshape(512, 512)

    tiles = call(seq_kernel, arr(8, 2, 80, 512), "seq", [ra, rb, rotated], [xh[None], y[None]])
    got = lax.all_to_all(tiles, ("xh", "y"), split_axis=0, concat_axis=0, tiled=True)
    seq_grads = call(sum_kernel, arr(2, 80, 1024), "sums", [got])

    sibling = shift(seq_grads, core=1)
    across = shift(seq_grads, xl=1)
    diagonal = shift(across, core=1)

    def score(grads):
        return jnp.einsum("sik,qik->sq", grads, query_grads, preferred_element_type=F32)

    scored = jnp.stack([score(seq_grads), score(sibling), score(across), score(diagonal)])
    here = xl * 2 + core
    scores = jnp.concatenate(
        [lax.dynamic_index_in_dim(scored, here ^ d, 0, keepdims=False) for d in range(4)], axis=0
    )
    return jnp.sum(spread(scores, ("z", "xh", "y"), 64), axis=0)


def solution(mesh):
    fine = Mesh(mesh.devices.reshape(2, 2, 8, 2, 4), ("xl", "core", "z", "xh", "y"))
    dp, eig = ("xl", "core"), ("z", "xh", "y")
    in_specs = (
        P(dp + eig, None),
        P(eig, dp),
        P(eig, None),
        P(eig, None),
        P(),
        P(dp),
        P(dp, eig, None),
    )
    return jax.shard_map(
        per_device, mesh=fine, in_specs=in_specs, out_specs=P(None, dp), check_vma=False
    )
```

```python
import jax
import jax.numpy as jnp
from jax import lax
from jax.experimental import pallas as pl
from jax.experimental.pallas import tpu as pltpu
from jax.sharding import Mesh, PartitionSpec as P

BLOCK = 128
LEN = 1024
BF = jnp.bfloat16
F32 = jnp.float32
SIZES = {"xl": 2, "core": 2, "z": 8, "xh": 2, "y": 4}
ROWS = (0, -1, 1, 2)
VMEM = pl.BlockSpec(memory_space=pltpu.VMEM)
SMEM = pl.BlockSpec(memory_space=pltpu.SMEM)
TINY = pl.CostEstimate(flops=1, bytes_accessed=1, transcendentals=0)
WIDE = pltpu.CompilerParams(vmem_limit_bytes=60 * 1024 * 1024)
ROOM = pltpu.CompilerParams(vmem_limit_bytes=10 * 1024 * 1024)


def shift(x, **by):
    axes = tuple(by)
    count = 1
    for a in axes:
        count *= SIZES[a]
    pairs = []
    for source in range(count):
        rest, target, scale = source, 0, 1
        for a in reversed(axes):
            target += (rest % SIZES[a] + by[a]) % SIZES[a] * scale
            rest //= SIZES[a]
            scale *= SIZES[a]
        pairs.append((source, target))
    return lax.ppermute(x, axes, pairs)


def spread(x, axes, count):
    return lax.all_to_all(
        jnp.broadcast_to(x[None], (count,) + x.shape), axes, split_axis=0, concat_axis=0, tiled=True
    )


def dot(a, b, ca, cb):
    return lax.dot_general(a, b, (((ca,), (cb,)), ((), ())), preferred_element_type=F32)


def reorder(y, g_ref, outs):
    lane = lax.broadcasted_iota(jnp.int32, (1, 128), 1) // 32
    for xh in range(2):
        for part in range(2):
            start = part * 1024 + xh * 128
            cols = [g_ref[:, start + j * 256 : start + j * 256 + 128].astype(F32) for j in range(4)]
            place = xh * 256 + part * 128
            for o_ref, off, dy in outs:
                total = None
                for j in range(4):
                    moved = pltpu.roll(cols[j], ((j - dy - y + 8) % 4) * 32, 1)
                    total = moved if total is None else jnp.where(lane == j, moved, total)
                o_ref[:, off + place : off + place + 128] = total.astype(BF)


def pick_kernel(ids, y_ref, core_ref, *refs):
    picked, g_ref, chosen, half, g0, g1, g2, g3 = refs[:8], *refs[8:]
    for n, p in enumerate(picked):
        chosen[:, n * 128 : n * 128 + 128] = p[...]
    half[...] = chosen[:, pl.ds(pl.multiple_of(core_ref[0] * 512, 128), 512)]
    reorder(y_ref[0], g_ref, ((g1, 0, 1), (g2, 0, -1), (g3, 0, 2), (g0, 0, 0)))


def pick(block_ids, y, core, basis_out, out_grads):
    rows, tokens = out_grads.shape
    whole = lambda width: pl.BlockSpec((rows, width), lambda g, *s: (0, 0))
    widths = (1024, 512, 512, 512, 512, 512)
    spec = pltpu.PrefetchScalarGridSpec(
        num_scalar_prefetch=3,
        grid=(1,),
        in_specs=[pl.BlockSpec((rows, BLOCK), lambda g, s, y, c, n=n: (0, s[n])) for n in range(8)] + [whole(tokens)],
        out_specs=[whole(w) for w in widths],
    )
    return pl.pallas_call(
        pick_kernel,
        grid_spec=spec,
        out_shape=[arr(rows, w) for w in widths],
        compiler_params=WIDE,
        name="pick",
    )(block_ids, y[None], core[None], *[basis_out] * 8, out_grads)


def halve_kernel(s_ref, b_ref, o_ref):
    o_ref[...] = b_ref[...]


def halve(core, basis_in):
    rows, half = basis_in.shape[0], basis_in.shape[1] // 2
    spec = pltpu.PrefetchScalarGridSpec(
        num_scalar_prefetch=1,
        grid=(1,),
        in_specs=[pl.BlockSpec((rows, half), lambda g, s: (0, s[0]))],
        out_specs=pl.BlockSpec((rows, half), lambda g, s: (0, 0)),
    )
    return pl.pallas_call(
        halve_kernel, grid_spec=spec, out_shape=arr(rows, half), compiler_params=ROOM, name="halve"
    )(core[None], basis_in)


def cut_kernel(core_ref, a_ref, *refs):
    o_ref = refs[-1]
    half = o_ref.shape[1]
    o_ref[...] = a_ref[:, pl.ds(pl.multiple_of((1 - core_ref[0]) * half, 128), half)]


def grads_kernel(core_ref, c0, h1, h2, h3, o1, o2, o3, g0, g1, g2, g3, b_own, b_far, o_ref, b0):
    b0[:80, :] = b_own[...]
    b0[80:, :] = b_far[...]
    for which, (a1, a2, a3) in ((core_ref[0], (h1, h2, h3)), (1 - core_ref[0], (o1, o2, o3))):
        for off in (0, 256):
            ks = slice(off, off + 256)
            place = pl.ds(pl.multiple_of(which * 512 + off, 256), 256)
            total = dot(c0[:, place], g0[...], 0, 0) + dot(a1[:, ks], g1[...], 0, 0)
            total += dot(a2[:, ks], g2[...], 0, 0) + dot(a3[:, ks], g3[...], 0, 0)
            o_ref[place, :] = total.astype(BF)


def live_kernel(y_ref, lens, parts, *refs):
    o_ref = refs[-1]
    total = parts[0].astype(F32)
    for n in range(1, 16):
        total += parts[n].astype(F32)
    col = lax.broadcasted_iota(jnp.int32, (1, 512), 1)
    pos = (col // 32 % 4) * 256 + col // 256 * 128 + y_ref[0] * 32 + col % 32
    limit = jnp.where(col % 256 < 128, lens[0], lens[1])
    total = jnp.where(pos < limit, total, 0.0).astype(BF)
    for n in range(8):
        o_ref[n] = total


def acts_kernel(core_ref, a_ref, sib, b0, b1, b2, b3a, b3b, aside, keep, send):
    half = sib.shape[1]
    mine = a_ref[:, pl.ds(pl.multiple_of(core_ref[0] * half, 128), half)]
    for tokens, out in ((sib[...], send), (mine, keep)):
        for n, b in enumerate((b0, b1, b2)):
            out[n * 160 : n * 160 + 160, :] = dot(b[...], tokens, 1, 1)
        out[480:, :] = dot(b3a[...], tokens[:, : half // 2], 1, 1) + dot(b3b[...], tokens[:, half // 2 :], 1, 1)


def add_kernel(a, b, o_ref):
    o_ref[...] = (a[...] + b[...]).astype(BF)


def seq_kernel(xh_ref, y_ref, ra, rb, rg, o_ref):
    xh = xh_ref[0]
    for s in range(2):
        near = rg[:, pl.ds(pl.multiple_of(xh * 256 + s * 128, 128), 128)]
        far = rg[:, pl.ds(pl.multiple_of((1 - xh) * 256 + s * 128, 128), 128)]
        cols = slice(s * 128, s * 128 + 128)
        right = jnp.concatenate([near, far], axis=1)
        for n, dy in enumerate(ROWS):
            for dx in range(2):
                mine = ra[n * 160 + dx * 80 : n * 160 + dx * 80 + 80, cols]
                other = rb[n * 160 + 80 - dx * 80 : n * 160 + 160 - dx * 80, cols]
                left = jnp.concatenate([mine, other], axis=1)
                target = (xh + dx) % 2 * 4 + (y_ref[0] + dy + 4) % 4
                o_ref[target, s] = dot(left, right, 1, 1).astype(BF)


def sum_kernel(parts, o_ref):
    for xh in range(2):
        total = parts[xh * 4].astype(F32)
        for y in range(1, 4):
            total += parts[xh * 4 + y].astype(F32)
        o_ref[:, :, xh * 512 : xh * 512 + 512] = total.astype(BF)


def call(kernel, out, name, args, scalars=(), aside=()):
    specs = [SMEM] * len(scalars) + [VMEM] * len(args) + [pl.BlockSpec(memory_space=pl.ANY)] * len(aside)
    return pl.pallas_call(
        kernel,
        out_shape=out,
        in_specs=specs,
        out_specs=jax.tree.map(lambda _: VMEM, out),
        compiler_params=ROOM,
        name=name,
        cost_estimate=TINY,
    )(*scalars, *args, *aside)


def arr(*shape):
    return jax.ShapeDtypeStruct(shape, BF)


def per_device(activations, out_grads, basis_in, basis_out, block_ids, seq_lens, query_grads):
    xl, core, xh, y = (lax.axis_index(a).astype(jnp.int32) for a in ("xl", "core", "xh", "y"))
    acts = lax.all_gather(activations, "z", axis=0, tiled=True)
    half = basis_in.shape[1] // 2
    chosen, c0, g0, g1, g2, g3 = pick(block_ids, y, core, basis_out, out_grads)
    c1, c2 = shift(c0, y=1), shift(c0, y=-1)
    g1, g2, g3 = shift(g1, y=1), shift(g2, y=-1), shift(g3, y=2)
    c3 = shift(c2, y=-1)
    others = [shift(c, core=1) for c in (c1, c2, c3)]
    b_own = halve(core, basis_in)
    b_far = shift(b_own, xl=1, xh=1)
    partial, b0 = call(
        grads_kernel,
        [arr(1024, 512), arr(160, half)],
        "grads",
        [chosen, c1, c2, c3, *others, g0, g1, g2, g3, b_own, b_far],
        [core[None]],
    )
    b1, b2 = shift(b0, y=1), shift(b0, y=-1)
    b3a, b3b = shift(b1[:, : half // 2], y=1), shift(b2[:, half // 2 :], y=-1)
    parts = lax.all_to_all(partial.reshape(16, 64, 512), ("xh", "z"), split_axis=0, concat_axis=0, tiled=True)
    copies = call(live_kernel, arr(8, 64, 512), "live", [parts], [y[None], seq_lens], [])
    wide = jax.ShapeDtypeStruct((640, 256), F32)
    sib = shift(call(cut_kernel, arr(256, half), "cut", [acts], [core[None]], [b1, b2]), core=1)
    keep, send = call(acts_kernel, [wide, wide], "acts", [acts, sib, b0, b1, b2, b3a, b3b], [core[None]], [copies])
    ra = call(add_kernel, arr(640, 256), "add", [keep, shift(send, core=1)])
    rb = shift(ra, xh=1)
    rotated = lax.all_to_all(copies, "z", split_axis=0, concat_axis=0, tiled=True).reshape(512, 512)

    tiles = call(seq_kernel, arr(8, 2, 80, 512), "seq", [ra, rb, rotated], [xh[None], y[None]])
    got = lax.all_to_all(tiles, ("xh", "y"), split_axis=0, concat_axis=0, tiled=True)
    seq_grads = call(sum_kernel, arr(2, 80, 1024), "sums", [got])

    sibling = shift(seq_grads, core=1)
    across = shift(seq_grads, xl=1)
    diagonal = shift(across, core=1)

    def score(grads):
        return jnp.einsum("sik,qik->sq", grads, query_grads, preferred_element_type=F32)

    scored = jnp.stack([score(seq_grads), score(sibling), score(across), score(diagonal)])
    here = xl * 2 + core
    scores = jnp.concatenate(
        [lax.dynamic_index_in_dim(scored, here ^ d, 0, keepdims=False) for d in range(4)], axis=0
    )
    return jnp.sum(spread(scores, ("z", "xh", "y"), 64), axis=0)


def solution(mesh):
    fine = Mesh(mesh.devices.reshape(2, 2, 8, 2, 4), ("xl", "core", "z", "xh", "y"))
    dp, eig = ("xl", "core"), ("z", "xh", "y")
    in_specs = (
        P(dp + eig, None),
        P(eig, dp),
        P(eig, None),
        P(eig, None),
        P(),
        P(dp),
        P(dp, eig, None),
    )
    return jax.shard_map(
        per_device, mesh=fine, in_specs=in_specs, out_specs=P(None, dp), check_vma=False
    )
```

```python
import jax
import jax.numpy as jnp
from jax import lax
from jax.experimental import pallas as pl
from jax.experimental.pallas import tpu as pltpu
from jax.sharding import Mesh, PartitionSpec as P

BLOCK = 128
LEN = 1024
BF = jnp.bfloat16
F32 = jnp.float32
SIZES = {"xl": 2, "core": 2, "z": 8, "xh": 2, "y": 4}
ROWS = (0, -1, 1, 2)
VMEM = pl.BlockSpec(memory_space=pltpu.VMEM)
SMEM = pl.BlockSpec(memory_space=pltpu.SMEM)
TINY = pl.CostEstimate(flops=1, bytes_accessed=1, transcendentals=0)
WIDE = pltpu.CompilerParams(vmem_limit_bytes=60 * 1024 * 1024)
ROOM = pltpu.CompilerParams(vmem_limit_bytes=10 * 1024 * 1024)


def shift(x, **by):
    axes = tuple(by)
    count = 1
    for a in axes:
        count *= SIZES[a]
    pairs = []
    for source in range(count):
        rest, target, scale = source, 0, 1
        for a in reversed(axes):
            target += (rest % SIZES[a] + by[a]) % SIZES[a] * scale
            rest //= SIZES[a]
            scale *= SIZES[a]
        pairs.append((source, target))
    return lax.ppermute(x, axes, pairs)


def spread(x, axes, count):
    return lax.all_to_all(
        jnp.broadcast_to(x[None], (count,) + x.shape), axes, split_axis=0, concat_axis=0, tiled=True
    )


def dot(a, b, ca, cb):
    return lax.dot_general(a, b, (((ca,), (cb,)), ((), ())), preferred_element_type=F32)


def reorder(y, g_ref, outs):
    lane = lax.broadcasted_iota(jnp.int32, (1, 128), 1) // 32
    for xh in range(2):
        for part in range(2):
            start = part * 1024 + xh * 128
            cols = [g_ref[:, start + j * 256 : start + j * 256 + 128].astype(F32) for j in range(4)]
            place = xh * 256 + part * 128
            for o_ref, off, dy in outs:
                total = None
                for j in range(4):
                    moved = pltpu.roll(cols[j], ((j - dy - y + 8) % 4) * 32, 1)
                    total = moved if total is None else jnp.where(lane == j, moved, total)
                o_ref[:, off + place : off + place + 128] = total.astype(BF)


def pick_kernel(ids, y_ref, core_ref, *refs):
    picked, g_ref, chosen, half, g0, g1, g2, g3 = refs[:8], *refs[8:]
    for n, p in enumerate(picked):
        chosen[:, n * 128 : n * 128 + 128] = p[...]
    half[...] = chosen[:, pl.ds(pl.multiple_of(core_ref[0] * 512, 128), 512)]
    reorder(y_ref[0], g_ref, ((g1, 0, 1), (g2, 0, -1), (g3, 0, 2), (g0, 0, 0)))


def pick(block_ids, y, core, basis_out, out_grads):
    rows, tokens = out_grads.shape
    whole = lambda width: pl.BlockSpec((rows, width), lambda g, *s: (0, 0))
    widths = (1024, 512, 512, 512, 512, 512)
    spec = pltpu.PrefetchScalarGridSpec(
        num_scalar_prefetch=3,
        grid=(1,),
        in_specs=[pl.BlockSpec((rows, BLOCK), lambda g, s, y, c, n=n: (0, s[n])) for n in range(8)] + [whole(tokens)],
        out_specs=[whole(w) for w in widths],
    )
    return pl.pallas_call(
        pick_kernel,
        grid_spec=spec,
        out_shape=[arr(rows, w) for w in widths],
        compiler_params=WIDE,
        name="pick",
    )(block_ids, y[None], core[None], *[basis_out] * 8, out_grads)


def halve_kernel(s_ref, b_ref, o_ref):
    o_ref[...] = b_ref[...]


def halve(core, basis_in):
    rows, half = basis_in.shape[0], basis_in.shape[1] // 2
    spec = pltpu.PrefetchScalarGridSpec(
        num_scalar_prefetch=1,
        grid=(1,),
        in_specs=[pl.BlockSpec((rows, half), lambda g, s: (0, s[0]))],
        out_specs=pl.BlockSpec((rows, half), lambda g, s: (0, 0)),
    )
    return pl.pallas_call(
        halve_kernel, grid_spec=spec, out_shape=arr(rows, half), compiler_params=ROOM, name="halve"
    )(core[None], basis_in)


def cut_kernel(core_ref, a_ref, *refs):
    o_ref = refs[-1]
    half = o_ref.shape[1]
    o_ref[...] = a_ref[:, pl.ds(pl.multiple_of((1 - core_ref[0]) * half, 128), half)]


def grads_kernel(core_ref, c0, h1, h2, h3, o1, o2, o3, g0, g1, g2, g3, b_own, b_far, o_ref, b0):
    b0[:80, :] = b_own[...]
    b0[80:, :] = b_far[...]
    for which, (a1, a2, a3) in ((core_ref[0], (h1, h2, h3)), (1 - core_ref[0], (o1, o2, o3))):
        for off in (0, 256):
            ks = slice(off, off + 256)
            place = pl.ds(pl.multiple_of(which * 512 + off, 256), 256)
            total = dot(c0[:, place], g0[...], 0, 0) + dot(a1[:, ks], g1[...], 0, 0)
            total += dot(a2[:, ks], g2[...], 0, 0) + dot(a3[:, ks], g3[...], 0, 0)
            o_ref[place, :] = total.astype(BF)


def live_kernel(y_ref, lens, parts, *refs):
    o_ref = refs[-1]
    total = parts[0].astype(F32)
    for n in range(1, 16):
        total += parts[n].astype(F32)
    col = lax.broadcasted_iota(jnp.int32, (1, 512), 1)
    pos = (col // 32 % 4) * 256 + col // 256 * 128 + y_ref[0] * 32 + col % 32
    limit = jnp.where(col % 256 < 128, lens[0], lens[1])
    total = jnp.where(pos < limit, total, 0.0).astype(BF)
    for n in range(8):
        o_ref[n] = total


def acts_kernel(core_ref, a_ref, sib, b0, b1, b2, b3a, b3b, keep, send):
    half = sib.shape[1]
    mine = a_ref[:, pl.ds(pl.multiple_of(core_ref[0] * half, 128), half)]
    for tokens, out in ((sib[...], send), (mine, keep)):
        for n, b in enumerate((b0, b1, b2)):
            out[n * 160 : n * 160 + 160, :] = dot(b[...], tokens, 1, 1)
        out[480:, :] = dot(b3a[...], tokens[:, : half // 2], 1, 1) + dot(b3b[...], tokens[:, half // 2 :], 1, 1)


def add_kernel(a, b, o_ref):
    o_ref[...] = (a[...] + b[...]).astype(BF)


def seq_kernel(xh_ref, y_ref, ra, rb, rg, o_ref):
    xh = xh_ref[0]
    for s in range(2):
        near = rg[:, pl.ds(pl.multiple_of(xh * 256 + s * 128, 128), 128)]
        far = rg[:, pl.ds(pl.multiple_of((1 - xh) * 256 + s * 128, 128), 128)]
        cols = slice(s * 128, s * 128 + 128)
        right = jnp.concatenate([near, far], axis=1)
        for n, dy in enumerate(ROWS):
            for dx in range(2):
                mine = ra[n * 160 + dx * 80 : n * 160 + dx * 80 + 80, cols]
                other = rb[n * 160 + 80 - dx * 80 : n * 160 + 160 - dx * 80, cols]
                left = jnp.concatenate([mine, other], axis=1)
                target = (xh + dx) % 2 * 4 + (y_ref[0] + dy + 4) % 4
                o_ref[target, s] = dot(left, right, 1, 1).astype(BF)


def sum_kernel(parts, o_ref):
    for xh in range(2):
        total = parts[xh * 4].astype(F32)
        for y in range(1, 4):
            total += parts[xh * 4 + y].astype(F32)
        o_ref[:, :, xh * 512 : xh * 512 + 512] = total.astype(BF)


def call(kernel, out, name, args, scalars=(), aside=()):
    specs = [SMEM] * len(scalars) + [VMEM] * len(args) + [pl.BlockSpec(memory_space=pl.ANY)] * len(aside)
    return pl.pallas_call(
        kernel,
        out_shape=out,
        in_specs=specs,
        out_specs=jax.tree.map(lambda _: VMEM, out),
        compiler_params=ROOM,
        name=name,
        cost_estimate=TINY,
    )(*scalars, *args, *aside)


def arr(*shape):
    return jax.ShapeDtypeStruct(shape, BF)


def per_device(activations, out_grads, basis_in, basis_out, block_ids, seq_lens, query_grads):
    xl, core, xh, y = (lax.axis_index(a).astype(jnp.int32) for a in ("xl", "core", "xh", "y"))
    acts = lax.all_gather(activations, "z", axis=0, tiled=True)
    half = basis_in.shape[1] // 2
    chosen, c0, g0, g1, g2, g3 = pick(block_ids, y, core, basis_out, out_grads)
    c1, c2 = shift(c0, y=1), shift(c0, y=-1)
    g1, g2, g3 = shift(g1, y=1), shift(g2, y=-1), shift(g3, y=2)
    c3 = shift(c2, y=-1)
    others = [shift(c, core=1) for c in (c1, c2, c3)]
    b_own = halve(core, basis_in)
    b_far = shift(b_own, xl=1, xh=1)
    partial, b0 = call(
        grads_kernel,
        [arr(1024, 512), arr(160, half)],
        "grads",
        [chosen, c1, c2, c3, *others, g0, g1, g2, g3, b_own, b_far],
        [core[None]],
    )
    b1, b2 = shift(b0, y=1), shift(b0, y=-1)
    b3a, b3b = shift(b1[:, : half // 2], y=1), shift(b2[:, half // 2 :], y=-1)
    parts = lax.all_to_all(partial.reshape(16, 64, 512), ("xh", "z"), split_axis=0, concat_axis=0, tiled=True)
    wide = jax.ShapeDtypeStruct((640, 256), F32)
    sib = shift(call(cut_kernel, arr(256, half), "cut", [acts], [core[None]], [b1, b2]), core=1)
    keep, send = call(acts_kernel, [wide, wide], "acts", [acts, sib, b0, b1, b2, b3a, b3b], [core[None]])
    ra = call(add_kernel, arr(640, 256), "add", [keep, shift(send, core=1)])
    rb = shift(ra, xh=1)
    copies = call(live_kernel, arr(8, 64, 512), "live", [parts], [y[None], seq_lens], [send])
    rotated = lax.all_to_all(copies, "z", split_axis=0, concat_axis=0, tiled=True).reshape(512, 512)

    tiles = call(seq_kernel, arr(8, 2, 80, 512), "seq", [ra, rb, rotated], [xh[None], y[None]])
    got = lax.all_to_all(tiles, ("xh", "y"), split_axis=0, concat_axis=0, tiled=True)
    seq_grads = call(sum_kernel, arr(2, 80, 1024), "sums", [got])

    sibling = shift(seq_grads, core=1)
    across = shift(seq_grads, xl=1)
    diagonal = shift(across, core=1)

    def score(grads):
        return jnp.einsum("sik,qik->sq", grads, query_grads, preferred_element_type=F32)

    scored = jnp.stack([score(seq_grads), score(sibling), score(across), score(diagonal)])
    here = xl * 2 + core
    scores = jnp.concatenate(
        [lax.dynamic_index_in_dim(scored, here ^ d, 0, keepdims=False) for d in range(4)], axis=0
    )
    return jnp.sum(spread(scores.reshape(1, 64), ("z", "xh", "y"), 64), axis=0).reshape(8, 8)


def solution(mesh):
    fine = Mesh(mesh.devices.reshape(2, 2, 8, 2, 4), ("xl", "core", "z", "xh", "y"))
    dp, eig = ("xl", "core"), ("z", "xh", "y")
    in_specs = (
        P(dp + eig, None),
        P(eig, dp),
        P(eig, None),
        P(eig, None),
        P(),
        P(dp),
        P(dp, eig, None),
    )
    return jax.shard_map(
        per_device, mesh=fine, in_specs=in_specs, out_specs=P(None, dp), check_vma=False
    )
```

```python
import jax
import jax.numpy as jnp
from jax import lax
from jax.experimental import pallas as pl
from jax.experimental.pallas import tpu as pltpu
from jax.sharding import Mesh, PartitionSpec as P

BLOCK = 128
LEN = 1024
BF = jnp.bfloat16
F32 = jnp.float32
SIZES = {"xl": 2, "core": 2, "z": 8, "xh": 2, "y": 4}
ROWS = (0, -1, 1, 2)
VMEM = pl.BlockSpec(memory_space=pltpu.VMEM)
SMEM = pl.BlockSpec(memory_space=pltpu.SMEM)
TINY = pl.CostEstimate(flops=1, bytes_accessed=1, transcendentals=0)
WIDE = pltpu.CompilerParams(vmem_limit_bytes=60 * 1024 * 1024)
ROOM = pltpu.CompilerParams(vmem_limit_bytes=10 * 1024 * 1024)


def shift(x, **by):
    axes = tuple(by)
    count = 1
    for a in axes:
        count *= SIZES[a]
    pairs = []
    for source in range(count):
        rest, target, scale = source, 0, 1
        for a in reversed(axes):
            target += (rest % SIZES[a] + by[a]) % SIZES[a] * scale
            rest //= SIZES[a]
            scale *= SIZES[a]
        pairs.append((source, target))
    return lax.ppermute(x, axes, pairs)


def spread(x, axes, count):
    return lax.all_to_all(
        jnp.broadcast_to(x[None], (count,) + x.shape), axes, split_axis=0, concat_axis=0, tiled=True
    )


def dot(a, b, ca, cb):
    return lax.dot_general(a, b, (((ca,), (cb,)), ((), ())), preferred_element_type=F32)


def reorder(y, g_ref, outs):
    lane = lax.broadcasted_iota(jnp.int32, (1, 128), 1) // 32
    for xh in range(2):
        for part in range(2):
            start = part * 1024 + xh * 128
            cols = [g_ref[:, start + j * 256 : start + j * 256 + 128].astype(F32) for j in range(4)]
            place = xh * 256 + part * 128
            for o_ref, off, dy in outs:
                total = None
                for j in range(4):
                    moved = pltpu.roll(cols[j], ((j - dy - y + 8) % 4) * 32, 1)
                    total = moved if total is None else jnp.where(lane == j, moved, total)
                o_ref[:, off + place : off + place + 128] = total.astype(BF)


def pick_kernel(ids, y_ref, core_ref, *refs):
    picked, g_ref, chosen, half, g0, g1, g2, g3 = refs[:8], *refs[8:]
    for n, p in enumerate(picked):
        chosen[:, n * 128 : n * 128 + 128] = p[...]
    half[...] = chosen[:, pl.ds(pl.multiple_of(core_ref[0] * 512, 128), 512)]
    reorder(y_ref[0], g_ref, ((g1, 0, 1), (g2, 0, -1), (g3, 0, 2), (g0, 0, 0)))


def pick(block_ids, y, core, basis_out, out_grads):
    rows, tokens = out_grads.shape
    whole = lambda width: pl.BlockSpec((rows, width), lambda g, *s: (0, 0))
    widths = (1024, 512, 512, 512, 512, 512)
    spec = pltpu.PrefetchScalarGridSpec(
        num_scalar_prefetch=3,
        grid=(1,),
        in_specs=[pl.BlockSpec((rows, BLOCK), lambda g, s, y, c, n=n: (0, s[n])) for n in range(8)] + [whole(tokens)],
        out_specs=[whole(w) for w in widths],
    )
    return pl.pallas_call(
        pick_kernel,
        grid_spec=spec,
        out_shape=[arr(rows, w) for w in widths],
        compiler_params=WIDE,
        name="pick",
    )(block_ids, y[None], core[None], *[basis_out] * 8, out_grads)


def halve_kernel(s_ref, b_ref, *refs):
    refs[-1][...] = b_ref[...]


def halve(which, x, aside=(), params=ROOM):
    rows, half = x.shape[0], x.shape[1] // 2
    spec = pltpu.PrefetchScalarGridSpec(
        num_scalar_prefetch=1,
        grid=(1,),
        in_specs=[pl.BlockSpec((rows, half), lambda g, s: (0, s[0]))]
        + [pl.BlockSpec(memory_space=pl.ANY)] * len(aside),
        out_specs=pl.BlockSpec((rows, half), lambda g, s: (0, 0)),
    )
    return pl.pallas_call(
        halve_kernel,
        grid_spec=spec,
        out_shape=arr(rows, half),
        compiler_params=params,
        cost_estimate=TINY,
        name="halve",
    )(which[None], x, *aside)


def grads_kernel(core_ref, c0, h1, h2, h3, o1, o2, o3, g0, g1, g2, g3, b_own, b_far, o_ref, b0):
    b0[:80, :] = b_own[...]
    b0[80:, :] = b_far[...]
    for which, (a1, a2, a3) in ((core_ref[0], (h1, h2, h3)), (1 - core_ref[0], (o1, o2, o3))):
        for off in (0, 256):
            ks = slice(off, off + 256)
            place = pl.ds(pl.multiple_of(which * 512 + off, 256), 256)
            total = dot(c0[:, place], g0[...], 0, 0) + dot(a1[:, ks], g1[...], 0, 0)
            total += dot(a2[:, ks], g2[...], 0, 0) + dot(a3[:, ks], g3[...], 0, 0)
            o_ref[place, :] = total.astype(BF)


def live_kernel(y_ref, lens, parts, *refs):
    o_ref = refs[-1]
    total = parts[0].astype(F32)
    for n in range(1, 16):
        total += parts[n].astype(F32)
    col = lax.broadcasted_iota(jnp.int32, (1, 512), 1)
    pos = (col // 32 % 4) * 256 + col // 256 * 128 + y_ref[0] * 32 + col % 32
    limit = jnp.where(col % 256 < 128, lens[0], lens[1])
    total = jnp.where(pos < limit, total, 0.0).astype(BF)
    for n in range(8):
        o_ref[n] = total


def acts_kernel(core_ref, a_ref, sib, b0, b1, b2, b3a, b3b, keep, send):
    half = sib.shape[1]
    mine = a_ref[:, pl.ds(pl.multiple_of(core_ref[0] * half, 128), half)]
    for tokens, out in ((sib[...], send), (mine, keep)):
        for n, b in enumerate((b0, b1, b2)):
            out[n * 160 : n * 160 + 160, :] = dot(b[...], tokens, 1, 1)
        out[480:, :] = dot(b3a[...], tokens[:, : half // 2], 1, 1) + dot(b3b[...], tokens[:, half // 2 :], 1, 1)


def add_kernel(a, b, o_ref):
    o_ref[...] = (a[...] + b[...]).astype(BF)


def seq_kernel(xh_ref, y_ref, ra, rb, rg, o_ref):
    xh = xh_ref[0]
    for s in range(2):
        near = rg[:, pl.ds(pl.multiple_of(xh * 256 + s * 128, 128), 128)]
        far = rg[:, pl.ds(pl.multiple_of((1 - xh) * 256 + s * 128, 128), 128)]
        cols = slice(s * 128, s * 128 + 128)
        right = jnp.concatenate([near, far], axis=1)
        for n, dy in enumerate(ROWS):
            for dx in range(2):
                mine = ra[n * 160 + dx * 80 : n * 160 + dx * 80 + 80, cols]
                other = rb[n * 160 + 80 - dx * 80 : n * 160 + 160 - dx * 80, cols]
                left = jnp.concatenate([mine, other], axis=1)
                target = (xh + dx) % 2 * 4 + (y_ref[0] + dy + 4) % 4
                o_ref[target, s] = dot(left, right, 1, 1).astype(BF)


def sum_kernel(parts, o_ref):
    for xh in range(2):
        total = parts[xh * 4].astype(F32)
        for y in range(1, 4):
            total += parts[xh * 4 + y].astype(F32)
        o_ref[:, :, xh * 512 : xh * 512 + 512] = total.astype(BF)


def call(kernel, out, name, args, scalars=(), aside=()):
    specs = [SMEM] * len(scalars) + [VMEM] * len(args) + [pl.BlockSpec(memory_space=pl.ANY)] * len(aside)
    return pl.pallas_call(
        kernel,
        out_shape=out,
        in_specs=specs,
        out_specs=jax.tree.map(lambda _: VMEM, out),
        compiler_params=ROOM,
        name=name,
        cost_estimate=TINY,
    )(*scalars, *args, *aside)


def arr(*shape):
    return jax.ShapeDtypeStruct(shape, BF)


def per_device(activations, out_grads, basis_in, basis_out, block_ids, seq_lens, query_grads):
    xl, core, xh, y = (lax.axis_index(a).astype(jnp.int32) for a in ("xl", "core", "xh", "y"))
    acts = lax.all_gather(activations, "z", axis=0, tiled=True)
    half = basis_in.shape[1] // 2
    chosen, c0, g0, g1, g2, g3 = pick(block_ids, y, core, basis_out, out_grads)
    c1, c2 = shift(c0, y=1), shift(c0, y=-1)
    g1, g2, g3 = shift(g1, y=1), shift(g2, y=-1), shift(g3, y=2)
    c3 = shift(c2, y=-1)
    others = [shift(c, core=1) for c in (c1, c2, c3)]
    b_own = halve(core, basis_in)
    b_far = shift(b_own, xl=1, xh=1)
    partial, b0 = call(
        grads_kernel,
        [arr(1024, 512), arr(160, half)],
        "grads",
        [chosen, c1, c2, c3, *others, g0, g1, g2, g3, b_own, b_far],
        [core[None]],
    )
    b1, b2 = shift(b0, y=1), shift(b0, y=-1)
    b3a, b3b = shift(b1[:, : half // 2], y=1), shift(b2[:, half // 2 :], y=-1)
    parts = lax.all_to_all(partial.reshape(16, 64, 512), ("xh", "z"), split_axis=0, concat_axis=0, tiled=True)
    wide = jax.ShapeDtypeStruct((640, 256), F32)
    sib = shift(halve(1 - core, acts, [b1, b2], pltpu.CompilerParams(vmem_limit_bytes=50 * 1024 * 1024)), core=1)
    keep, send = call(acts_kernel, [wide, wide], "acts", [acts, sib, b0, b1, b2, b3a, b3b], [core[None]])
    ra = call(add_kernel, arr(640, 256), "add", [keep, shift(send, core=1)])
    rb = shift(ra, xh=1)
    copies = call(live_kernel, arr(8, 64, 512), "live", [parts], [y[None], seq_lens], [send])
    rotated = lax.all_to_all(copies, "z", split_axis=0, concat_axis=0, tiled=True).reshape(512, 512)

    tiles = call(seq_kernel, arr(8, 2, 80, 512), "seq", [ra, rb, rotated], [xh[None], y[None]])
    got = lax.all_to_all(tiles, ("xh", "y"), split_axis=0, concat_axis=0, tiled=True)
    seq_grads = call(sum_kernel, arr(2, 80, 1024), "sums", [got])

    sibling = shift(seq_grads, core=1)
    across = shift(seq_grads, xl=1)
    diagonal = shift(across, core=1)

    def score(grads):
        return jnp.einsum("sik,qik->sq", grads, query_grads, preferred_element_type=F32)

    scored = jnp.stack([score(seq_grads), score(sibling), score(across), score(diagonal)])
    here = xl * 2 + core
    scores = jnp.concatenate(
        [lax.dynamic_index_in_dim(scored, here ^ d, 0, keepdims=False) for d in range(4)], axis=0
    )
    return jnp.sum(spread(scores.reshape(1, 64), ("z", "xh", "y"), 64), axis=0).reshape(8, 8)


def solution(mesh):
    fine = Mesh(mesh.devices.reshape(2, 2, 8, 2, 4), ("xl", "core", "z", "xh", "y"))
    dp, eig = ("xl", "core"), ("z", "xh", "y")
    in_specs = (
        P(dp + eig, None),
        P(eig, dp),
        P(eig, None),
        P(eig, None),
        P(),
        P(dp),
        P(dp, eig, None),
    )
    return jax.shard_map(
        per_device, mesh=fine, in_specs=in_specs, out_specs=P(None, dp), check_vma=False
    )
```
